512 devices in a mesh: fsdp: 16 (over x_lo, y), dp: 32 (over x_hi, z, core).
Axes of the slice: x: 4 (x_hi: 2, x_lo: 2; x = x_hi * 2 + x_lo), y: 8, z: 8, core: 2. Of those that a mesh axis runs over, the one named last changes fastest.
Arguments:
- attn_out: bfloat16 [32768, 8192], P('dp', 'fsdp'), may hold values from -6 to 6
- key_cotangent: bfloat16 [32768, 1024], P('dp'), may hold values from -6 to 6
- key_weight: bfloat16 [8192, 1024], P('fsdp'), may hold values from -0.0625 to 0.0625
- proj_in: bfloat16 [64, 8192], P(None, 'fsdp'), may hold values from -0.0625 to 0.0625
- proj_out: bfloat16 [64, 8192], P(None, 'fsdp'), may hold values from -0.0625 to 0.0625
- query_sketches: bfloat16 [32, 128, 4096], P('dp', 'fsdp'), may hold values from -6 to 6
- block_owner: int32 [32], replicated, may hold values from 0 to 31, each once
- example_ids: int32 [32, 1024], P('dp'), may hold values from 0 to 15, never falling along the last dimension, each value on 1 to 96 neighbouring positions
Outputs:
- scores: float32 [512, 32, 128], P('dp', None, 'fsdp')
The draws below stay inside these ranges and needn't reach their ends.
Inputs may be any that keep to these rules, and one draw needn't show every extreme that they name: `block_owner`: names every dp index exactly once. `example_ids`: each row numbers the examples of a dp block in order, each 1 to 96 tokens.
All inputs are finite; a program needn't handle non-finite values.
Results may differ from the reference program's by a relative error of at most 0.0003.
Values may be sent and summed in bfloat16 or wider, within the bound.
A program may use at most 64 MiB of HBM per device.

```python
import math
import jax
import jax.numpy as jnp
import numpy as np
from jax import lax

D = 8192
KV = 1024
R = 64
TOK_DP = 1024
QB = 128
SKETCH_ENTRIES = 4096
EX = 16
MOST = 96
TOKENS = 32768
TRAIN_EXAMPLES = 512
N_DP = 32


def steps_of(key, shape, cuts, low, high):
    level, own = 1.0, jax.random.fold_in(key, 6)
    for position, shards_of in cuts:
        draws = jnp.exp(jax.random.uniform(jax.random.fold_in(own, position), (shards_of,), jnp.float32, low / len(cuts), high / len(cuts)))
        level = level * jnp.repeat(draws, shape[position] // shards_of).reshape([-1 if axis == position else 1 for axis in range(len(shape))])
    return level


def profile(number_of, total, bound, slope):
    loads = [(1 << 20) // math.isqrt(rank ** slope) + 1 for rank in range(2, number_of + 1)]
    surplus, given = total - bound - (number_of - 1), [1] * (number_of - 1)
    while surplus > 0:
        candidates = [i for i in range(number_of - 1) if given[i] < bound]
        pool, left = sum([loads[i] for i in candidates]), surplus
        for i in candidates:
            more = min(bound - given[i], max(1, left * loads[i] // pool), surplus)
            given[i] = given[i] + more
            surplus = surplus - more
    return np.array([bound] + given)


def ragged(rng, count, total, bound, skew):
    if count == 2:
        one = jax.random.randint(rng, (), max(1, total - bound), min(bound, total - 1) + 1)
        return jnp.stack([one, total - one])
    tallies = jnp.asarray(profile(count, total, bound, skew), jnp.int32)
    couples = (count - 1) // 2
    donor, receiver = tallies[1:1 + 2 * couples:2], tallies[2:2 + 2 * couples:2]
    slack = jnp.minimum(donor - 1, bound - receiver)
    passed = jax.random.randint(jax.random.fold_in(rng, 1), (couples,), 0, 1 << 20) % (slack + 1)
    tallies = tallies.at[1:1 + 2 * couples:2].set(donor - passed).at[2:2 + 2 * couples:2].set(receiver + passed)
    return tallies[jax.random.permutation(jax.random.fold_in(rng, 2), count)]


def scatter_about(rng, shape, spread, limit, split=(), held_as=jnp.bfloat16):
    drawn = jax.random.normal(rng, shape, jnp.float32) * spread
    if len(split) > 0:
        drawn = steps_of(rng, shape, split, -0.22, 0.18) * drawn
    return jnp.clip(drawn, min=-limit, max=limit).astype(held_as)


def setup_inputs(seed: int = 0) -> dict:
    key_of = jax.random.split(jax.random.key(seed), 9)
    return {
        "attn_out": scatter_about(key_of[0], (TOKENS, D), 1.0, 6.0, ((0, 32), (1, 16))),
        "key_cotangent": scatter_about(key_of[1], (TOKENS, KV), 1.0, 6.0, ((0, 32),)),
        "key_weight": scatter_about(key_of[2], (D, KV), D ** -0.5, 0.0625, ((0, 16),)),
        "proj_in": scatter_about(key_of[3], (R, D), D ** -0.5, 0.0625, ((1, 16),)),
        "proj_out": scatter_about(key_of[4], (R, D), D ** -0.5, 0.0625, ((1, 16),)),
        "query_sketches": scatter_about(key_of[5], (N_DP, QB, SKETCH_ENTRIES), 1.0, 6.0, ((0, 32), (1, 16))),
        "block_owner": jax.random.permutation(key_of[6], N_DP).astype(jnp.int32),
        "example_ids": jax.vmap(lambda own: jnp.searchsorted(jnp.cumsum(ragged(own, EX, TOK_DP, MOST, 1)), jnp.arange(TOK_DP), side="right"))(jax.random.split(key_of[7], N_DP)).reshape((N_DP, TOK_DP)).astype(jnp.int32),
    }


def damped_inverse(gram):
    size = gram.shape[0]
    eye = jnp.eye(size, dtype=jnp.float32)
    damped = gram + 0.1 * jnp.trace(gram) / size * eye
    factor = jnp.linalg.cholesky(damped)
    return jax.scipy.linalg.cho_solve((factor, True), eye)

def reference(attn_out, key_cotangent, key_weight, proj_in, proj_out, query_sketches, block_owner, example_ids):
    acts = attn_out.reshape(N_DP, TOK_DP, D)
    cots = key_cotangent.reshape(N_DP, TOK_DP, KV)
    out_factor = proj_out.astype(jnp.float32)
    labels = jnp.arange(EX, dtype=jnp.int32)

    def one_block(inputs):
        act, cot, ids = inputs
        u_rows = jnp.dot(act.astype(jnp.float32), proj_in.T.astype(jnp.float32), preferred_element_type=jnp.float32)
        grad_out = jnp.dot(cot.astype(jnp.float32), key_weight.T.astype(jnp.float32), preferred_element_type=jnp.float32)
        v_rows = jnp.dot(grad_out, out_factor.T, precision=lax.Precision.HIGHEST)
        onehot = (ids[None, :] == labels[:, None]).astype(jnp.float32)
        weighted_sketch = onehot[:, :, None] * v_rows[None, :, :]
        sketch = jnp.einsum('eti,tj->eij', weighted_sketch, u_rows, precision=lax.Precision.HIGHEST)
        gin = jnp.dot(u_rows.T, u_rows, precision=lax.Precision.HIGHEST)
        gout = jnp.dot(v_rows.T, v_rows, precision=lax.Precision.HIGHEST)
        return (sketch, gin, gout)
    sketches, gins, gouts = lax.map(one_block, (acts, cots, example_ids))
    inv_in = damped_inverse(jnp.sum(gins, axis=0) / TOKENS)
    inv_out = damped_inverse(jnp.sum(gouts, axis=0) / TOKENS)
    sketches = sketches.reshape(TRAIN_EXAMPLES, R, R)
    preconditioner = jnp.einsum('ik,nkl,lj->nij', inv_out, sketches, inv_in, precision=lax.Precision.HIGHEST)
    sorted_scores = query_sketches[block_owner].astype(jnp.float32)
    scores = jnp.einsum('hd,xyd->hxy', preconditioner.reshape(TRAIN_EXAMPLES, SKETCH_ENTRIES), sorted_scores, precision=lax.Precision.HIGHEST)
    return scores / SKETCH_ENTRIES
```

```python
import functools
import jax
import jax.numpy as jnp
from jax import lax
from jax.experimental import pallas as pl
from jax.experimental.pallas import tpu as pltpu
from jax.sharding import PartitionSpec as P

EX = 16
R = 64
LANES = 128
MESH = pl.DeviceIdType.MESH
NT = (((1,), (1,)), ((), ()))
F32 = jnp.float32
BF16 = jnp.bfloat16


def exact(a, b, dims=(((1,), (0,)), ((), ()))):
    return lax.dot_general(a, b, dims, precision=lax.Precision.HIGHEST, preferred_element_type=F32)


def bf_dot(a, b, dims=(((1,), (0,)), ((), ()))):
    return lax.dot_general(a, b, dims, preferred_element_type=F32)


def halves(x):
    high = x.astype(BF16)
    return high, (x - high.astype(F32)).astype(BF16)


def inverse_pair(gram, eye, left_half, scale):
    diag = jnp.sum(gram * eye, axis=0, keepdims=True) * scale
    tr_in = jnp.sum(jnp.where(left_half, diag, 0.0), axis=1, keepdims=True)
    tr_out = jnp.sum(jnp.where(left_half, 0.0, diag), axis=1, keepdims=True)
    bound = jnp.where(left_half, tr_in, tr_out) * (1.0 + 0.1 / R)
    low = (0.1 / R) / (1.0 + 0.1 / R)
    mat = gram * (scale / bound) + low * eye
    start = 2.0 / (1.0 + low)
    rho = (1.0 - low) / (1.0 + low)
    gain = 2.0 / (2.0 - rho * rho)
    rho = rho * rho / (2.0 - rho * rho)
    prod = start * mat
    turn = 2.0 * eye - prod
    inv = (gain * start) * turn
    prod = gain * exact(prod, turn)
    while rho > 0.05:
        gain = 2.0 / (2.0 - rho * rho)
        rho = rho * rho / (2.0 - rho * rho)
        turn = 2.0 * eye - prod
        both = exact(jnp.concatenate([prod, inv], axis=0), turn) * gain
        prod, inv = both[:LANES], both[LANES:]
    for _ in range(2):
        inv = exact(inv, 2.0 * eye - exact(mat, inv))
    return inv / bound


def kernel(
    nf, nd, tokens_all,
    attn_hbm, cot_hbm, kw_hbm, pin_ref, pout_ref, query_ref, owner_ref, ids_ref,
    out_ref,
    attn, cot, kw, part, rs_buf, chunks, gram_part, ga_buf, gb_own, gb_buf, gfull, qall, select, flat, stage,
    load_sem, rs_send, rs_recv, ag_send, ag_recv, ga_send, ga_recv, gb_send, gb_recv, gc_send, gc_recv,
    q_send, q_recv, sib_send, sib_recv,
):
    f = lax.axis_index("fsdp")
    j = lax.axis_index("dp")
    ntb = nf // 2
    nch = nd // 2
    rows = R // ntb
    core, chip = lax.rem(j, 2), j // 2
    side, block = lax.rem(f, 2), f // 2

    load_attn = pltpu.make_async_copy(attn_hbm, attn, load_sem.at[0])
    load_kw = pltpu.make_async_copy(kw_hbm, kw, load_sem.at[1])
    load_cot = pltpu.make_async_copy(cot_hbm, cot, load_sem.at[2])
    load_attn.start()
    load_kw.start()
    load_cot.start()

    barrier = pltpu.get_barrier_semaphore()

    @pl.loop(1, nf)
    def _(r):
        pl.semaphore_signal(barrier, inc=1, device_id={"fsdp": lax.rem(f + r, nf)}, device_id_type=MESH)

    @pl.loop(1, nd)
    def _(r):
        pl.semaphore_signal(barrier, inc=1, device_id={"dp": lax.rem(j + r, nd)}, device_id_type=MESH)

    half = query_ref.shape[2] // 2
    per = query_ref.shape[1]
    own_q = query_ref[0]
    qall[core, chip] = jnp.concatenate([own_q[:, :half], own_q[:, half:]], axis=0)

    owner = jnp.concatenate([owner_ref[...]] * per, axis=1)
    cols = lax.broadcasted_iota(jnp.int32, select.shape, 1)
    rws = lax.broadcasted_iota(jnp.int32, select.shape, 0)
    holder = lax.rem(rws // (2 * per), nch) * 2 + rws // (2 * per * nch)
    hit = jnp.logical_and(holder == owner, lax.rem(rws, per) == cols // nd)
    select[...] = hit.astype(F32).astype(BF16)

    def scatter(which):
        @pl.loop(0, ntb)
        def _(t):
            dst = 2 * t + which
            slot = lax.rem(dst - f + nf, nf)

            @pl.when(slot > 0)
            def _():
                pltpu.make_async_remote_copy(
                    src_ref=part.at[dst], dst_ref=rs_buf.at[slot - 1], send_sem=rs_send, recv_sem=rs_recv,
                    device_id={"fsdp": dst}, device_id_type=MESH,
                ).start()

    load_attn.wait()
    u_part = bf_dot(pin_ref[...], attn[...], NT)
    for t in range(ntb):
        part[2 * t] = u_part[:, LANES * t:LANES * (t + 1)]
    pl.semaphore_wait(barrier, nf - 1 + nd - 1)
    scatter(0)

    load_kw.wait()
    w_part = bf_dot(pout_ref[...], kw[...])
    w_two = jnp.concatenate(halves(w_part), axis=0)
    load_cot.wait()
    v_two = bf_dot(w_two, cot[...], NT)
    v_part = v_two[:R] + v_two[R:]
    for t in range(ntb):
        part[2 * t + 1] = v_part[:, LANES * t:LANES * (t + 1)]
    scatter(1)

    @pl.loop(1, nch)
    def _(r):
        pltpu.make_async_remote_copy(
            src_ref=qall.at[core, chip], dst_ref=qall.at[core, chip], send_sem=q_send, recv_sem=q_recv,
            device_id={"dp": lax.rem(j + 2 * r, nd)}, device_id_type=MESH,
        ).start()

    row_id = lax.broadcasted_iota(jnp.int32, (LANES, LANES), 0)
    col_id = lax.broadcasted_iota(jnp.int32, (LANES, LANES), 1)
    eye = (row_id == col_id).astype(F32)
    left_half = lax.broadcasted_iota(jnp.int32, (1, LANES), 1) < R

    pltpu.make_async_copy(rs_buf, rs_buf, rs_recv).wait()
    mine = part[f]
    for r in range(nf - 1):
        mine = mine + rs_buf[r]
    chunks[f] = mine

    @pl.loop(1, nf)
    def _(r):
        pltpu.make_async_remote_copy(
            src_ref=chunks.at[f], dst_ref=chunks.at[f], send_sem=ag_send, recv_sem=ag_recv,
            device_id={"fsdp": lax.rem(f + r, nf)}, device_id_type=MESH,
        ).start()

    zero = jnp.zeros_like(mine)
    wide = jnp.concatenate([jnp.where(side == 0, mine, zero), jnp.where(side == 0, zero, mine)], axis=0)
    gram = exact(mine, wide, NT)
    for t in range(ntb):
        gram_part[t] = gram[rows * t:rows * (t + 1)]

    @pl.loop(1, ntb)
    def _(r):
        to = lax.rem(block + r, ntb)
        pltpu.make_async_remote_copy(
            src_ref=gram_part.at[to], dst_ref=ga_buf.at[r - 1], send_sem=ga_send, recv_sem=ga_recv,
            device_id={"fsdp": 2 * to + side}, device_id_type=MESH,
        ).start()

    pltpu.make_async_copy(ga_buf, ga_buf, ga_recv).wait()
    gsum = gram_part[block]
    for r in range(ntb - 1):
        gsum = gsum + ga_buf[r]
    gb_own[...] = gsum

    @pl.loop(1, nd)
    def _(r):
        pltpu.make_async_remote_copy(
            src_ref=gb_own, dst_ref=gb_buf.at[r - 1], send_sem=gb_send, recv_sem=gb_recv,
            device_id={"dp": lax.rem(j + r, nd)}, device_id_type=MESH,
        ).start()

    pltpu.make_async_copy(gb_buf, gb_buf, gb_recv).wait()
    for r in range(nd - 1):
        gsum = gsum + gb_buf[r]
    place = side * ntb + block
    gfull[place] = gsum

    @pl.loop(1, nf)
    def _(r):
        pltpu.make_async_remote_copy(
            src_ref=gfull.at[place], dst_ref=gfull.at[place], send_sem=gc_send, recv_sem=gc_recv,
            device_id={"fsdp": lax.rem(f + r, nf)}, device_id_type=MESH,
        ).start()

    others = qall.at[0, pl.ds(0, nch - 1)]
    pltpu.make_async_copy(others, others, q_recv).wait()
    sibling = pltpu.make_async_remote_copy(
        src_ref=qall.at[core], dst_ref=qall.at[core], send_sem=sib_send, recv_sem=sib_recv,
        device_id={"dp": j + 1 - 2 * core}, device_id_type=MESH,
    )
    sibling.start()

    all_chunks = chunks.at[pl.ds(0, nf - 1)]
    pltpu.make_async_copy(all_chunks, all_chunks, ag_recv).wait()
    u_high, u_low = halves(jnp.concatenate([chunks[2 * t] for t in range(ntb)], axis=1))
    v_high, v_low = halves(jnp.concatenate([chunks[2 * t + 1] for t in range(ntb)], axis=1))
    v_both = jnp.concatenate([v_high, v_low], axis=0)
    ids = ids_ref[...]
    none = jnp.zeros_like(u_high)
    pair = EX // 2
    for p in range(pair):
        marks = [jnp.broadcast_to(ids == e, u_high.shape) for e in (p, p + pair)]
        masked_high = jnp.concatenate([jnp.where(m, u_high, none) for m in marks], axis=0)
        masked_low = jnp.concatenate([jnp.where(m, u_low, none) for m in marks], axis=0)
        top = bf_dot(v_both, masked_high, NT)
        stage[pl.ds(R * p, R), :] = top[:R] + top[R:] + bf_dot(v_high, masked_low, NT)

    all_grams = gfull.at[pl.ds(0, nf - 1)]
    pltpu.make_async_copy(all_grams, all_grams, gc_recv).wait()
    inv = inverse_pair(jnp.concatenate([gfull[t] for t in range(nf)], axis=0), eye, left_half, 1.0 / tokens_all)
    corner = jnp.where(jnp.logical_and(row_id < R, col_id < R), inv, 0.0)
    twice = corner + pltpu.roll(pltpu.roll(corner, R, 0), R, 1)
    right = exact(stage[...], twice)
    right = jnp.concatenate([right[R * p:R * (p + 1)] for p in range(pair)], axis=1)
    both = exact(inv[R:], jnp.concatenate([right, right], axis=0))
    for p in range(pair):
        stage[pl.ds(R * p, R), :] = both[:, LANES * p:LANES * (p + 1)]
    for i in range(R // 2):
        a = stage[pl.ds(2 * i, pair, stride=R), :]
        b = stage[pl.ds(2 * i + 1, pair, stride=R), :]
        low = jnp.where(left_half, a, pltpu.roll(b, R, 1))
        high = jnp.where(left_half, pltpu.roll(a, R, 1), b)
        big, small = halves(jnp.concatenate([low, high], axis=0))
        top, left = (2 * i * R) // half * 2 * EX, (2 * i * R) % half
        flat[pl.ds(top, EX), pl.ds(left, LANES)] = big
        flat[pl.ds(top + EX, EX), pl.ds(left, LANES)] = small

    sibling.wait_recv()
    raw = bf_dot(flat[...], qall[...].reshape(nd * 2 * per, half), NT)
    first = raw[:EX] + raw[EX:2 * EX]
    second = raw[2 * EX:3 * EX] + raw[3 * EX:]
    column = lax.broadcasted_iota(jnp.int32, first.shape, 1)
    sums = jnp.where(lax.rem(column // per, 2) == 0, first, second)
    big = sums.astype(BF16)
    rest = sums - big.astype(F32)
    mid = rest.astype(BF16)
    tail = (rest - mid.astype(F32)).astype(BF16)
    picked = bf_dot(jnp.concatenate([big, mid, tail], axis=0), select[...])
    out_ref[...] = (picked[:EX] + picked[EX:2 * EX] + picked[2 * EX:]) * (1.0 / (R * R))

    sibling.wait_send()
    pltpu.make_async_copy(rs_buf, rs_buf, rs_send).wait()
    pltpu.make_async_copy(all_chunks, all_chunks, ag_send).wait()
    pltpu.make_async_copy(ga_buf, ga_buf, ga_send).wait()
    pltpu.make_async_copy(gb_buf, gb_buf, gb_send).wait()
    pltpu.make_async_copy(all_grams, all_grams, gc_send).wait()
    pltpu.make_async_copy(others, others, q_send).wait()


def on_device(
    nf, nd, attn_out, key_cotangent, key_weight, proj_in, proj_out, query_sketches, block_owner, example_ids
):
    tokens = attn_out.shape[0]
    per = query_sketches.shape[1]
    half = query_sketches.shape[2] // 2
    ntb = nf // 2
    rows = R // ntb
    hbm = pl.BlockSpec(memory_space=pl.ANY)
    vmem = pl.BlockSpec(memory_space=pltpu.VMEM)
    scores = pl.pallas_call(
        functools.partial(kernel, nf, nd, nd * tokens),
        out_shape=jax.ShapeDtypeStruct((EX, per * nd), F32),
        in_specs=[hbm, hbm, hbm, vmem, vmem, vmem, vmem, vmem],
        out_specs=vmem,
        scratch_shapes=[
            pltpu.VMEM(attn_out.shape, BF16),
            pltpu.VMEM(key_cotangent.shape, BF16),
            pltpu.VMEM(key_weight.shape, BF16),
            pltpu.VMEM((nf, R, LANES), F32),
            pltpu.VMEM((nf - 1, R, LANES), F32),
            pltpu.VMEM((nf, R, LANES), F32),
            pltpu.VMEM((ntb, rows, LANES), F32),
            pltpu.VMEM((ntb - 1, rows, LANES), F32),
            pltpu.VMEM((rows, LANES), F32),
            pltpu.VMEM((nd - 1, rows, LANES), F32),
            pltpu.VMEM((nf, rows, LANES), F32),
            pltpu.VMEM((2, nd // 2, 2 * per, half), BF16),
            pltpu.VMEM((nd * 2 * per, per * nd), BF16),
            pltpu.VMEM((4 * EX, half), BF16),
            pltpu.VMEM((EX // 2 * R, LANES), F32),
            pltpu.SemaphoreType.DMA((3,)),
        ] + [pltpu.SemaphoreType.DMA] * 14,
        compiler_params=pltpu.CompilerParams(
            collective_id=0, has_side_effects=True, vmem_limit_bytes=40 * 1024 * 1024
        ),
        name="influence",
    )(
        attn_out, key_cotangent, key_weight, proj_in, proj_out, query_sketches,
        block_owner.reshape(1, nd), example_ids,
    )
    return scores.reshape(EX, per, nd).transpose(0, 2, 1)


def solution(mesh):
    return jax.shard_map(
        functools.partial(on_device, mesh.shape["fsdp"], mesh.shape["dp"]),
        mesh=mesh,
        in_specs=(
            P("dp", "fsdp"),
            P("dp", None),
            P("fsdp", None),
            P(None, "fsdp"),
            P(None, "fsdp"),
            P("dp", "fsdp", None),
            P(),
            P("dp", None),
        ),
        out_specs=P("dp", None, "fsdp"),
        check_vma=False,
    )
```

```python
import functools
import jax
import jax.numpy as jnp
from jax import lax
from jax.experimental import pallas as pl
from jax.experimental.pallas import tpu as pltpu
from jax.sharding import PartitionSpec as P

EX = 16
R = 64
LANES = 128
MESH = pl.DeviceIdType.MESH
NT = (((1,), (1,)), ((), ()))
F32 = jnp.float32
BF16 = jnp.bfloat16


def exact(a, b, dims=(((1,), (0,)), ((), ()))):
    return lax.dot_general(a, b, dims, precision=lax.Precision.HIGHEST, preferred_element_type=F32)


def bf_dot(a, b, dims=(((1,), (0,)), ((), ()))):
    return lax.dot_general(a, b, dims, preferred_element_type=F32)


def halves(x):
    high = x.astype(BF16)
    return high, (x - high.astype(F32)).astype(BF16)


def inverse_pair(gram, eye, left_half, scale):
    diag = jnp.sum(gram * eye, axis=0, keepdims=True) * scale
    tr_in = jnp.sum(jnp.where(left_half, diag, 0.0), axis=1, keepdims=True)
    tr_out = jnp.sum(jnp.where(left_half, 0.0, diag), axis=1, keepdims=True)
    bound = jnp.where(left_half, tr_in, tr_out) * (1.0 + 0.1 / R)
    low = (0.1 / R) / (1.0 + 0.1 / R)
    mat = gram * (scale / bound) + low * eye
    start = 2.0 / (1.0 + low)
    rho = (1.0 - low) / (1.0 + low)
    gain = 2.0 / (2.0 - rho * rho)
    rho = rho * rho / (2.0 - rho * rho)
    prod = start * mat
    turn = 2.0 * eye - prod
    inv = (gain * start) * turn
    prod = gain * exact(prod, turn)
    while rho > 0.05:
        gain = 2.0 / (2.0 - rho * rho)
        rho = rho * rho / (2.0 - rho * rho)
        turn = 2.0 * eye - prod
        both = exact(jnp.concatenate([prod, inv], axis=0), turn) * gain
        prod, inv = both[:LANES], both[LANES:]
    for _ in range(2):
        inv = exact(inv, 2.0 * eye - exact(mat, inv))
    return inv / bound


def kernel(
    nf, nd, tokens_all,
    attn_hbm, cot_hbm, kw_hbm, pin_hbm, pout_hbm, query_hbm, owner_hbm, ids_hbm,
    out_ref,
    attn, cot, kw, pin_ref, pout_ref, query_ref, owner_ref, ids_ref, part, rs_buf, chunks, gram_part, ga_buf, gb_own, gb_buf, gfull, qall, select, flat, stage,
    load_sem, rs_send, rs_recv, ag_send, ag_recv, ga_send, ga_recv, gb_send, gb_recv, gc_send, gc_recv,
    q_send, q_recv, sib_send, sib_recv,
):
    f = lax.axis_index("fsdp")
    j = lax.axis_index("dp")
    ntb = nf // 2
    nch = nd // 2
    rows = R // ntb
    core, chip = lax.rem(j, 2), j // 2
    side, block = lax.rem(f, 2), f // 2

    load_attn = pltpu.make_async_copy(attn_hbm, attn, load_sem.at[0])
    load_pin = pltpu.make_async_copy(pin_hbm, pin_ref, load_sem.at[1])
    load_kw = pltpu.make_async_copy(kw_hbm, kw, load_sem.at[2])
    load_pout = pltpu.make_async_copy(pout_hbm, pout_ref, load_sem.at[3])
    load_cot = pltpu.make_async_copy(cot_hbm, cot, load_sem.at[4])
    load_query = pltpu.make_async_copy(query_hbm, query_ref, load_sem.at[5])
    load_owner = pltpu.make_async_copy(owner_hbm, owner_ref, load_sem.at[6])
    load_ids = pltpu.make_async_copy(ids_hbm, ids_ref, load_sem.at[7])
    for load in (load_attn, load_pin, load_kw, load_pout, load_cot, load_query, load_owner, load_ids):
        load.start()

    barrier = pltpu.get_barrier_semaphore()

    @pl.loop(1, nf)
    def _(r):
        pl.semaphore_signal(barrier, inc=1, device_id={"fsdp": lax.rem(f + r, nf)}, device_id_type=MESH)

    @pl.loop(1, nd)
    def _(r):
        pl.semaphore_signal(barrier, inc=1, device_id={"dp": lax.rem(j + r, nd)}, device_id_type=MESH)

    half = query_ref.shape[2] // 2
    per = query_ref.shape[1]
    load_query.wait()
    load_owner.wait()
    own_q = query_ref[0]
    qall[core, chip] = jnp.concatenate([own_q[:, :half], own_q[:, half:]], axis=0)

    owner = jnp.concatenate([owner_ref[...]] * per, axis=1)
    cols = lax.broadcasted_iota(jnp.int32, select.shape, 1)
    rws = lax.broadcasted_iota(jnp.int32, select.shape, 0)
    holder = lax.rem(rws // (2 * per), nch) * 2 + rws // (2 * per * nch)
    hit = jnp.logical_and(holder == owner, lax.rem(rws, per) == cols // nd)
    select[...] = hit.astype(F32).astype(BF16)

    def scatter(which):
        @pl.loop(0, ntb)
        def _(t):
            dst = 2 * t + which
            slot = lax.rem(dst - f + nf, nf)

            @pl.when(slot > 0)
            def _():
                pltpu.make_async_remote_copy(
                    src_ref=part.at[dst], dst_ref=rs_buf.at[slot - 1], send_sem=rs_send, recv_sem=rs_recv,
                    device_id={"fsdp": dst}, device_id_type=MESH,
                ).start()

    load_attn.wait()
    load_pin.wait()
    u_part = bf_dot(pin_ref[...], attn[...], NT)
    for t in range(ntb):
        part[2 * t] = u_part[:, LANES * t:LANES * (t + 1)]
    pl.semaphore_wait(barrier, nf - 1 + nd - 1)
    scatter(0)

    load_kw.wait()
    load_pout.wait()
    w_part = bf_dot(pout_ref[...], kw[...])
    w_two = jnp.concatenate(halves(w_part), axis=0)
    load_cot.wait()
    v_two = bf_dot(w_two, cot[...], NT)
    v_part = v_two[:R] + v_two[R:]
    for t in range(ntb):
        part[2 * t + 1] = v_part[:, LANES * t:LANES * (t + 1)]
    scatter(1)

    @pl.loop(1, nch)
    def _(r):
        pltpu.make_async_remote_copy(
            src_ref=qall.at[core, chip], dst_ref=qall.at[core, chip], send_sem=q_send, recv_sem=q_recv,
            device_id={"dp": lax.rem(j + 2 * r, nd)}, device_id_type=MESH,
        ).start()

    row_id = lax.broadcasted_iota(jnp.int32, (LANES, LANES), 0)
    col_id = lax.broadcasted_iota(jnp.int32, (LANES, LANES), 1)
    eye = (row_id == col_id).astype(F32)
    left_half = lax.broadcasted_iota(jnp.int32, (1, LANES), 1) < R

    pltpu.make_async_copy(rs_buf, rs_buf, rs_recv).wait()
    mine = part[f]
    for r in range(nf - 1):
        mine = mine + rs_buf[r]
    chunks[f] = mine

    @pl.loop(1, nf)
    def _(r):
        pltpu.make_async_remote_copy(
            src_ref=chunks.at[f], dst_ref=chunks.at[f], send_sem=ag_send, recv_sem=ag_recv,
            device_id={"fsdp": lax.rem(f + r, nf)}, device_id_type=MESH,
        ).start()

    zero = jnp.zeros_like(mine)
    wide = jnp.concatenate([jnp.where(side == 0, mine, zero), jnp.where(side == 0, zero, mine)], axis=0)
    gram = exact(mine, wide, NT)
    for t in range(ntb):
        gram_part[t] = gram[rows * t:rows * (t + 1)]

    @pl.loop(1, ntb)
    def _(r):
        to = lax.rem(block + r, ntb)
        pltpu.make_async_remote_copy(
            src_ref=gram_part.at[to], dst_ref=ga_buf.at[r - 1], send_sem=ga_send, recv_sem=ga_recv,
            device_id={"fsdp": 2 * to + side}, device_id_type=MESH,
        ).start()

    pltpu.make_async_copy(ga_buf, ga_buf, ga_recv).wait()
    gsum = gram_part[block]
    for r in range(ntb - 1):
        gsum = gsum + ga_buf[r]
    gb_own[...] = gsum

    @pl.loop(1, nd)
    def _(r):
        pltpu.make_async_remote_copy(
            src_ref=gb_own, dst_ref=gb_buf.at[r - 1], send_sem=gb_send, recv_sem=gb_recv,
            device_id={"dp": lax.rem(j + r, nd)}, device_id_type=MESH,
        ).start()

    pltpu.make_async_copy(gb_buf, gb_buf, gb_recv).wait()
    for r in range(nd - 1):
        gsum = gsum + gb_buf[r]
    place = side * ntb + block
    gfull[place] = gsum

    @pl.loop(1, nf)
    def _(r):
        pltpu.make_async_remote_copy(
            src_ref=gfull.at[place], dst_ref=gfull.at[place], send_sem=gc_send, recv_sem=gc_recv,
            device_id={"fsdp": lax.rem(f + r, nf)}, device_id_type=MESH,
        ).start()

    others = qall.at[0, pl.ds(0, nch - 1)]
    pltpu.make_async_copy(others, others, q_recv).wait()
    sibling = pltpu.make_async_remote_copy(
        src_ref=qall.at[core], dst_ref=qall.at[core], send_sem=sib_send, recv_sem=sib_recv,
        device_id={"dp": j + 1 - 2 * core}, device_id_type=MESH,
    )
    sibling.start()

    all_chunks = chunks.at[pl.ds(0, nf - 1)]
    pltpu.make_async_copy(all_chunks, all_chunks, ag_recv).wait()
    u_high, u_low = halves(jnp.concatenate([chunks[2 * t] for t in range(ntb)], axis=1))
    v_high, v_low = halves(jnp.concatenate([chunks[2 * t + 1] for t in range(ntb)], axis=1))
    v_both = jnp.concatenate([v_high, v_low], axis=0)
    load_ids.wait()
    ids = ids_ref[...]
    none = jnp.zeros_like(u_high)
    pair = EX // 2
    for p in range(pair):
        marks = [jnp.broadcast_to(ids == e, u_high.shape) for e in (p, p + pair)]
        masked_high = jnp.concatenate([jnp.where(m, u_high, none) for m in marks], axis=0)
        masked_low = jnp.concatenate([jnp.where(m, u_low, none) for m in marks], axis=0)
        top = bf_dot(v_both, masked_high, NT)
        stage[pl.ds(R * p, R), :] = top[:R] + top[R:] + bf_dot(v_high, masked_low, NT)

    all_grams = gfull.at[pl.ds(0, nf - 1)]
    pltpu.make_async_copy(all_grams, all_grams, gc_recv).wait()
    inv = inverse_pair(jnp.concatenate([gfull[t] for t in range(nf)], axis=0), eye, left_half, 1.0 / tokens_all)
    corner = jnp.where(jnp.logical_and(row_id < R, col_id < R), inv, 0.0)
    twice = corner + pltpu.roll(pltpu.roll(corner, R, 0), R, 1)
    right = exact(stage[...], twice)
    right = jnp.concatenate([right[R * p:R * (p + 1)] for p in range(pair)], axis=1)
    both = exact(inv[R:], jnp.concatenate([right, right], axis=0))
    for p in range(pair):
        stage[pl.ds(R * p, R), :] = both[:, LANES * p:LANES * (p + 1)]
    for i in range(R // 2):
        a = stage[pl.ds(2 * i, pair, stride=R), :]
        b = stage[pl.ds(2 * i + 1, pair, stride=R), :]
        low = jnp.where(left_half, a, pltpu.roll(b, R, 1))
        high = jnp.where(left_half, pltpu.roll(a, R, 1), b)
        big, small = halves(jnp.concatenate([low, high], axis=0))
        top, left = (2 * i * R) // half * 2 * EX, (2 * i * R) % half
        flat[pl.ds(top, EX), pl.ds(left, LANES)] = big
        flat[pl.ds(top + EX, EX), pl.ds(left, LANES)] = small

    sibling.wait_recv()
    raw = bf_dot(flat[...], qall[...].reshape(nd * 2 * per, half), NT)
    first = raw[:EX] + raw[EX:2 * EX]
    second = raw[2 * EX:3 * EX] + raw[3 * EX:]
    column = lax.broadcasted_iota(jnp.int32, first.shape, 1)
    sums = jnp.where(lax.rem(column // per, 2) == 0, first, second)
    big = sums.astype(BF16)
    rest = sums - big.astype(F32)
    mid = rest.astype(BF16)
    tail = (rest - mid.astype(F32)).astype(BF16)
    picked = bf_dot(jnp.concatenate([big, mid, tail], axis=0), select[...])
    out_ref[...] = (picked[:EX] + picked[EX:2 * EX] + picked[2 * EX:]) * (1.0 / (R * R))

    sibling.wait_send()
    pltpu.make_async_copy(rs_buf, rs_buf, rs_send).wait()
    pltpu.make_async_copy(all_chunks, all_chunks, ag_send).wait()
    pltpu.make_async_copy(ga_buf, ga_buf, ga_send).wait()
    pltpu.make_async_copy(gb_buf, gb_buf, gb_send).wait()
    pltpu.make_async_copy(all_grams, all_grams, gc_send).wait()
    pltpu.make_async_copy(others, others, q_send).wait()


def on_device(
    nf, nd, attn_out, key_cotangent, key_weight, proj_in, proj_out, query_sketches, block_owner, example_ids
):
    tokens = attn_out.shape[0]
    per = query_sketches.shape[1]
    half = query_sketches.shape[2] // 2
    ntb = nf // 2
    rows = R // ntb
    hbm = pl.BlockSpec(memory_space=pl.ANY)
    vmem = pl.BlockSpec(memory_space=pltpu.VMEM)
    scores = pl.pallas_call(
        functools.partial(kernel, nf, nd, nd * tokens),
        out_shape=jax.ShapeDtypeStruct((EX, per * nd), F32),
        in_specs=[hbm] * 8,
        out_specs=vmem,
        scratch_shapes=[
            pltpu.VMEM(attn_out.shape, BF16),
            pltpu.VMEM(key_cotangent.shape, BF16),
            pltpu.VMEM(key_weight.shape, BF16),
            pltpu.VMEM(proj_in.shape, BF16),
            pltpu.VMEM(proj_out.shape, BF16),
            pltpu.VMEM(query_sketches.shape, BF16),
            pltpu.VMEM((1, nd), jnp.int32),
            pltpu.VMEM(example_ids.shape, jnp.int32),
            pltpu.VMEM((nf, R, LANES), F32),
            pltpu.VMEM((nf - 1, R, LANES), F32),
            pltpu.VMEM((nf, R, LANES), F32),
            pltpu.VMEM((ntb, rows, LANES), F32),
            pltpu.VMEM((ntb - 1, rows, LANES), F32),
            pltpu.VMEM((rows, LANES), F32),
            pltpu.VMEM((nd - 1, rows, LANES), F32),
            pltpu.VMEM((nf, rows, LANES), F32),
            pltpu.VMEM((2, nd // 2, 2 * per, half), BF16),
            pltpu.VMEM((nd * 2 * per, per * nd), BF16),
            pltpu.VMEM((4 * EX, half), BF16),
            pltpu.VMEM((EX // 2 * R, LANES), F32),
            pltpu.SemaphoreType.DMA((8,)),
        ] + [pltpu.SemaphoreType.DMA] * 14,
        compiler_params=pltpu.CompilerParams(
            collective_id=0, has_side_effects=True, vmem_limit_bytes=62 * 1024 * 1024
        ),
        name="influence",
    )(
        attn_out, key_cotangent, key_weight, proj_in, proj_out, query_sketches,
        block_owner.reshape(1, nd), example_ids,
    )
    return scores.reshape(EX, per, nd).transpose(0, 2, 1)


def solution(mesh):
    return jax.shard_map(
        functools.partial(on_device, mesh.shape["fsdp"], mesh.shape["dp"]),
        mesh=mesh,
        in_specs=(
            P("dp", "fsdp"),
            P("dp", None),
            P("fsdp", None),
            P(None, "fsdp"),
            P(None, "fsdp"),
            P("dp", "fsdp", None),
            P(),
            P("dp", None),
        ),
        out_specs=P("dp", None, "fsdp"),
        check_vma=False,
    )
```

```python
import functools
import jax
import jax.numpy as jnp
from jax import lax
from jax.experimental import pallas as pl
from jax.experimental.pallas import tpu as pltpu
from jax.sharding import PartitionSpec as P

EX = 16
R = 64
LANES = 128
MESH = pl.DeviceIdType.MESH
NT = (((1,), (1,)), ((), ()))
F32 = jnp.float32
BF16 = jnp.bfloat16


def exact(a, b, dims=(((1,), (0,)), ((), ()))):
    return lax.dot_general(a, b, dims, precision=lax.Precision.HIGHEST, preferred_element_type=F32)


def bf_dot(a, b, dims=(((1,), (0,)), ((), ()))):
    return lax.dot_general(a, b, dims, preferred_element_type=F32)


def halves(x):
    high = x.astype(BF16)
    return high, (x - high.astype(F32)).astype(BF16)


def inverse_pair(gram, eye, left_half, scale):
    diag = jnp.sum(gram * eye, axis=0, keepdims=True) * scale
    tr_in = jnp.sum(jnp.where(left_half, diag, 0.0), axis=1, keepdims=True)
    tr_out = jnp.sum(jnp.where(left_half, 0.0, diag), axis=1, keepdims=True)
    bound = jnp.where(left_half, tr_in, tr_out) * (1.0 + 0.1 / R)
    low = (0.1 / R) / (1.0 + 0.1 / R)
    mat = gram * (scale / bound) + low * eye
    start = 2.0 / (1.0 + low)
    rho = (1.0 - low) / (1.0 + low)
    gain = 2.0 / (2.0 - rho * rho)
    rho = rho * rho / (2.0 - rho * rho)
    prod = start * mat
    turn = 2.0 * eye - prod
    inv = (gain * start) * turn
    prod = gain * exact(prod, turn)
    while rho > 0.05:
        gain = 2.0 / (2.0 - rho * rho)
        rho = rho * rho / (2.0 - rho * rho)
        turn = 2.0 * eye - prod
        both = exact(jnp.concatenate([prod, inv], axis=0), turn) * gain
        prod, inv = both[:LANES], both[LANES:]
    for _ in range(2):
        inv = exact(inv, 2.0 * eye - exact(mat, inv))
    return inv / bound


def by_distance(steps, far):
    return sorted(steps, key=lambda r: -far(r))


def kernel(
    nf, nd, tokens_all,
    attn_hbm, cot_hbm, kw_hbm, pin_hbm, pout_hbm, query_hbm, owner_hbm, ids_hbm,
    out_ref,
    attn, cot, kw, pin_ref, pout_ref, query_ref, owner_ref, ids_ref, part, rs_buf, chunks, gram_part, ga_buf, gs_buf, gb_own, gb_buf, gfull, qall, select, flat, stage,
    load_sem, *sems,
):
    rs_sems, ag_sems, ga_sems, gs_sems, gb_sems, gc_sems, x_sems, q_sems, p_sems, sib_sems = zip(sems[::2], sems[1::2])
    f = lax.axis_index("fsdp")
    j = lax.axis_index("dp")
    ntb = nf // 2
    nch = nd // 2
    rows = R // ntb
    core, chip = lax.rem(j, 2), j // 2
    side, block = lax.rem(f, 2), f // 2
    half = query_ref.shape[2] // 2
    per = query_ref.shape[1]

    load_attn = pltpu.make_async_copy(attn_hbm, attn, load_sem.at[0])
    load_pin = pltpu.make_async_copy(pin_hbm, pin_ref, load_sem.at[1])
    load_kw = pltpu.make_async_copy(kw_hbm, kw, load_sem.at[2])
    load_pout = pltpu.make_async_copy(pout_hbm, pout_ref, load_sem.at[3])
    load_cot = pltpu.make_async_copy(cot_hbm, cot, load_sem.at[4])
    load_query = pltpu.make_async_copy(query_hbm, query_ref, load_sem.at[5])
    load_owner = pltpu.make_async_copy(owner_hbm, owner_ref, load_sem.at[6])
    load_ids = pltpu.make_async_copy(ids_hbm, ids_ref, load_sem.at[7])
    for load in (load_attn, load_pin, load_kw, load_pout, load_cot, load_query, load_owner, load_ids):
        load.start()

    ny, nz = nf // 2, nd // 4
    f_far = lambda r: min(r % ny, ny - r % ny) + (r >= ny)
    z_far = lambda r: min(r % nz, nz - r % nz) + 2 * (r >= nz)
    f_steps = by_distance(range(1, nf), f_far)
    d_steps = by_distance(range(1, nch), z_far)
    sibling = {"dp": j + 1 - 2 * core}
    over_f = lambda r: {"fsdp": lax.rem(f + r, nf)}
    over_d = lambda r: {"dp": lax.rem(j + 2 * r, nd)}

    barrier = pltpu.get_barrier_semaphore()
    for peer in [over_d(r) for r in d_steps] + [over_f(r) for r in f_steps] + [sibling]:
        pl.semaphore_signal(barrier, inc=1, device_id=peer, device_id_type=MESH)

    def send(src, dst, sems, peer):
        copy = pltpu.make_async_remote_copy(
            src_ref=src, dst_ref=dst, send_sem=sems[0], recv_sem=sems[1], device_id=peer, device_id_type=MESH
        )
        copy.start()
        return copy

    even = by_distance(range(0, nf, 2), f_far)
    odd = by_distance(range(1, nf, 2), f_far)
    even = [r for r in even if r] + [0]

    def scatter(which):
        other = side != which
        for r_even, r_odd in zip(even, odd):
            r = jnp.where(other, r_odd, r_even)
            dst = lax.rem(f + r, nf)

            @pl.when(r > 0)
            def _():
                send(part.at[dst], rs_buf.at[r - 1], rs_sems, {"fsdp": dst})

    load_attn.wait()
    load_pin.wait()
    u_part = bf_dot(pin_ref[...], attn[...], NT)
    for t in range(ntb):
        part[2 * t] = u_part[:, LANES * t:LANES * (t + 1)]
    pl.semaphore_wait(barrier, nf - 1 + nch)
    scatter(0)

    load_kw.wait()
    load_pout.wait()
    w_part = bf_dot(pout_ref[...], kw[...])
    w_two = jnp.concatenate(halves(w_part), axis=0)
    load_cot.wait()
    v_two = bf_dot(w_two, cot[...], NT)
    v_part = v_two[:R] + v_two[R:]
    for t in range(ntb):
        part[2 * t + 1] = v_part[:, LANES * t:LANES * (t + 1)]
    scatter(1)

    load_query.wait()
    own_q = query_ref[0]
    z, x = lax.rem(chip, nz), chip // nz
    partner = 1 - x
    qall[core, z, x] = jnp.concatenate([own_q[:, :half], own_q[:, half:]], axis=0)
    across = send(qall.at[core, z, x], qall.at[core, z, x], x_sems, {"dp": lax.rem(j + nch, nd)})
    z_steps = by_distance(range(1, nz), z_far)
    along_z = lambda r: {"dp": (x * nz + lax.rem(z + r, nz)) * 2 + core}
    for r in z_steps:
        send(qall.at[core, z, x], qall.at[core, z, x], q_sems, along_z(r))

    load_owner.wait()
    owner = jnp.concatenate([owner_ref[...]] * per, axis=1)
    cols = lax.broadcasted_iota(jnp.int32, select.shape, 1)
    rws = lax.broadcasted_iota(jnp.int32, select.shape, 0)
    block_of = rws // (2 * per)
    holder = (lax.rem(block_of, 2) * nz + lax.rem(block_of // 2, nz)) * 2 + block_of // nch
    hit = jnp.logical_and(holder == owner, lax.rem(rws, per) == cols // nd)
    select[...] = hit.astype(F32).astype(BF16)

    across.wait_recv()
    for r in z_steps:
        send(qall.at[core, z, partner], qall.at[core, z, partner], p_sems, along_z(r))

    row_id = lax.broadcasted_iota(jnp.int32, (LANES, LANES), 0)
    col_id = lax.broadcasted_iota(jnp.int32, (LANES, LANES), 1)
    eye = (row_id == col_id).astype(F32)
    left_half = lax.broadcasted_iota(jnp.int32, (1, LANES), 1) < R

    pltpu.make_async_copy(rs_buf, rs_buf, rs_sems[1]).wait()
    mine = part[f]
    for r in range(nf - 1):
        mine = mine + rs_buf[r]
    chunks[f] = mine

    zero = jnp.zeros_like(mine)
    wide = jnp.concatenate([jnp.where(side == 0, mine, zero), jnp.where(side == 0, zero, mine)], axis=0)
    gram = exact(mine, wide, NT)
    for t in range(ntb):
        gram_part[t] = gram[rows * t:rows * (t + 1)]

    for r in by_distance(range(1, ntb), lambda r: f_far(2 * r)):
        to = lax.rem(block + r, ntb)
        send(gram_part.at[to], ga_buf.at[r - 1], ga_sems, {"fsdp": 2 * to + side})
    for r in f_steps:
        send(chunks.at[f], chunks.at[f], ag_sems, over_f(r))

    pltpu.make_async_copy(ga_buf, ga_buf, ga_sems[1]).wait()
    gsum = gram_part[block]
    for r in range(ntb - 1):
        gsum = gsum + ga_buf[r]
    gb_own[0] = gsum
    twin = send(gb_own.at[0], gs_buf, gs_sems, sibling)
    twin.wait_recv()
    gsum = gsum + gs_buf[...]
    gb_own[1] = gsum
    for r in d_steps:
        send(gb_own.at[1], gb_buf.at[r - 1], gb_sems, over_d(r))

    pltpu.make_async_copy(gb_buf, gb_buf, gb_sems[1]).wait()
    for r in range(nch - 1):
        gsum = gsum + gb_buf[r]
    place = side * ntb + block
    gfull[place] = gsum

    for r in f_steps:
        send(gfull.at[place], gfull.at[place], gc_sems, over_f(r))

    blocks = qall.at[0, pl.ds(0, nz - 1), 0]
    pltpu.make_async_copy(blocks, blocks, q_sems[1]).wait()
    pltpu.make_async_copy(blocks, blocks, p_sems[1]).wait()
    twin_q = send(qall.at[core], qall.at[core], sib_sems, sibling)

    all_chunks = chunks.at[pl.ds(0, nf - 1)]
    pltpu.make_async_copy(all_chunks, all_chunks, ag_sems[1]).wait()
    u_high, u_low = halves(jnp.concatenate([chunks[2 * t] for t in range(ntb)], axis=1))
    v_high, v_low = halves(jnp.concatenate([chunks[2 * t + 1] for t in range(ntb)], axis=1))
    v_both = jnp.concatenate([v_high, v_low], axis=0)
    load_ids.wait()
    ids = ids_ref[...]
    none = jnp.zeros_like(u_high)
    pair = EX // 2
    for p in range(pair):
        marks = [jnp.broadcast_to(ids == e, u_high.shape) for e in (p, p + pair)]
        masked_high = jnp.concatenate([jnp.where(m, u_high, none) for m in marks], axis=0)
        masked_low = jnp.concatenate([jnp.where(m, u_low, none) for m in marks], axis=0)
        top = bf_dot(v_both, masked_high, NT)
        stage[pl.ds(R * p, R), :] = top[:R] + top[R:] + bf_dot(v_high, masked_low, NT)

    all_grams = gfull.at[pl.ds(0, nf - 1)]
    pltpu.make_async_copy(all_grams, all_grams, gc_sems[1]).wait()
    inv = inverse_pair(jnp.concatenate([gfull[t] for t in range(nf)], axis=0), eye, left_half, 1.0 / tokens_all)
    corner = jnp.where(jnp.logical_and(row_id < R, col_id < R), inv, 0.0)
    twice = corner + pltpu.roll(pltpu.roll(corner, R, 0), R, 1)
    right = exact(stage[...], twice)
    right = jnp.concatenate([right[R * p:R * (p + 1)] for p in range(pair)], axis=1)
    both = exact(inv[R:], jnp.concatenate([right, right], axis=0))
    for p in range(pair):
        stage[pl.ds(R * p, R), :] = both[:, LANES * p:LANES * (p + 1)]
    for i in range(R // 2):
        a = stage[pl.ds(2 * i, pair, stride=R), :]
        b = stage[pl.ds(2 * i + 1, pair, stride=R), :]
        low = jnp.where(left_half, a, pltpu.roll(b, R, 1))
        high = jnp.where(left_half, pltpu.roll(a, R, 1), b)
        big, small = halves(jnp.concatenate([low, high], axis=0))
        top, left = (2 * i * R) // half * 2 * EX, (2 * i * R) % half
        flat[pl.ds(top, EX), pl.ds(left, LANES)] = big
        flat[pl.ds(top + EX, EX), pl.ds(left, LANES)] = small

    twin_q.wait_recv()
    raw = bf_dot(flat[...], qall[...].reshape(nd * 2 * per, half), NT)
    first = raw[:EX] + raw[EX:2 * EX]
    second = raw[2 * EX:3 * EX] + raw[3 * EX:]
    column = lax.broadcasted_iota(jnp.int32, first.shape, 1)
    sums = jnp.where(lax.rem(column // per, 2) == 0, first, second)
    big = sums.astype(BF16)
    rest = sums - big.astype(F32)
    mid = rest.astype(BF16)
    tail = (rest - mid.astype(F32)).astype(BF16)
    picked = bf_dot(jnp.concatenate([big, mid, tail], axis=0), select[...])
    picked = (picked[:EX] + picked[EX:2 * EX] + picked[2 * EX:]) * (1.0 / (R * R))
    for i in range(per):
        out_ref[:, i, :] = picked[:, nd * i:nd * (i + 1)]

    across.wait_send()
    twin.wait_send()
    twin_q.wait_send()
    for buf, sems in (
        (rs_buf, rs_sems), (all_chunks, ag_sems), (ga_buf, ga_sems), (gb_buf, gb_sems), (all_grams, gc_sems),
        (blocks, q_sems), (blocks, p_sems),
    ):
        pltpu.make_async_copy(buf, buf, sems[0]).wait()


def on_device(
    nf, nd, attn_out, key_cotangent, key_weight, proj_in, proj_out, query_sketches, block_owner, example_ids
):
    tokens = attn_out.shape[0]
    per = query_sketches.shape[1]
    half = query_sketches.shape[2] // 2
    ntb = nf // 2
    rows = R // ntb
    hbm = pl.BlockSpec(memory_space=pl.ANY)
    vmem = pl.BlockSpec(memory_space=pltpu.VMEM)
    scores = pl.pallas_call(
        functools.partial(kernel, nf, nd, nd * tokens),
        out_shape=jax.ShapeDtypeStruct((EX, per, nd), F32),
        in_specs=[hbm] * 8,
        out_specs=vmem,
        scratch_shapes=[
            pltpu.VMEM(attn_out.shape, BF16),
            pltpu.VMEM(key_cotangent.shape, BF16),
            pltpu.VMEM(key_weight.shape, BF16),
            pltpu.VMEM(proj_in.shape, BF16),
            pltpu.VMEM(proj_out.shape, BF16),
            pltpu.VMEM(query_sketches.shape, BF16),
            pltpu.VMEM((1, nd), jnp.int32),
            pltpu.VMEM(example_ids.shape, jnp.int32),
            pltpu.VMEM((nf, R, LANES), F32),
            pltpu.VMEM((nf - 1, R, LANES), F32),
            pltpu.VMEM((nf, R, LANES), F32),
            pltpu.VMEM((ntb, rows, LANES), F32),
            pltpu.VMEM((ntb - 1, rows, LANES), F32),
            pltpu.VMEM((rows, LANES), F32),
            pltpu.VMEM((2, rows, LANES), F32),
            pltpu.VMEM((nd // 2 - 1, rows, LANES), F32),
            pltpu.VMEM((nf, rows, LANES), F32),
            pltpu.VMEM((2, nd // 4, 2, 2 * per, half), BF16),
            pltpu.VMEM((nd * 2 * per, per * nd), BF16),
            pltpu.VMEM((4 * EX, half), BF16),
            pltpu.VMEM((EX // 2 * R, LANES), F32),
            pltpu.SemaphoreType.DMA((8,)),
        ] + [pltpu.SemaphoreType.DMA] * 20,
        compiler_params=pltpu.CompilerParams(
            collective_id=0, has_side_effects=True, vmem_limit_bytes=62 * 1024 * 1024
        ),
        name="influence",
    )(
        attn_out, key_cotangent, key_weight, proj_in, proj_out, query_sketches,
        block_owner.reshape(1, nd), example_ids,
    )
    return scores.transpose(0, 2, 1)


def solution(mesh):
    return jax.shard_map(
        functools.partial(on_device, mesh.shape["fsdp"], mesh.shape["dp"]),
        mesh=mesh,
        in_specs=(
            P("dp", "fsdp"),
            P("dp", None),
            P("fsdp", None),
            P(None, "fsdp"),
            P(None, "fsdp"),
            P("dp", "fsdp", None),
            P(),
            P("dp", None),
        ),
        out_specs=P("dp", None, "fsdp"),
        check_vma=False,
    )
```

```python
import functools
import jax
import jax.numpy as jnp
from jax import lax
from jax.experimental import pallas as pl
from jax.experimental.pallas import tpu as pltpu
from jax.sharding import PartitionSpec as P

EX = 16
R = 64
LANES = 128
MESH = pl.DeviceIdType.MESH
NT = (((1,), (1,)), ((), ()))
F32 = jnp.float32
BF16 = jnp.bfloat16


def exact(a, b, dims=(((1,), (0,)), ((), ()))):
    return lax.dot_general(a, b, dims, precision=lax.Precision.HIGHEST, preferred_element_type=F32)


def bf_dot(a, b, dims=(((1,), (0,)), ((), ()))):
    return lax.dot_general(a, b, dims, preferred_element_type=F32)


def halves(x):
    high = x.astype(BF16)
    return high, (x - high.astype(F32)).astype(BF16)


def three(a, b):
    a_high, a_low = halves(a)
    b_high, b_low = halves(b)
    return bf_dot(jnp.concatenate([a_high, a_low, a_high], axis=1), jnp.concatenate([b_high, b_high, b_low], axis=0))


def split_ring(n):
    near = [d for d in (n - 2, 2, n - 1, 1) if 0 < d < n]
    near = sorted(set(near), key=near.index)
    return near, [d for d in (n // 2, n // 2 - 1, n // 2 + 1) if 0 < d < n and d not in near]


def inverse_pair(gram, eye, left_half, scale):
    diag = jnp.sum(gram * eye, axis=0, keepdims=True) * scale
    tr_in = jnp.sum(jnp.where(left_half, diag, 0.0), axis=1, keepdims=True)
    tr_out = jnp.sum(jnp.where(left_half, 0.0, diag), axis=1, keepdims=True)
    bound = jnp.where(left_half, tr_in, tr_out) * (1.0 + 0.1 / R)
    low = (0.1 / R) / (1.0 + 0.1 / R)
    mat = gram * (scale / bound) + low * eye
    start = 2.0 / (1.0 + low)
    rho = (1.0 - low) / (1.0 + low)
    gain = 2.0 / (2.0 - rho * rho)
    rho = rho * rho / (2.0 - rho * rho)
    prod = start * mat
    turn = 2.0 * eye - prod
    inv = (gain * start) * turn
    prod = gain * three(prod, turn)
    while rho > 0.05:
        gain = 2.0 / (2.0 - rho * rho)
        rho = rho * rho / (2.0 - rho * rho)
        turn = 2.0 * eye - prod
        both = three(jnp.concatenate([prod, inv], axis=0), turn) * gain
        prod, inv = both[:LANES], both[LANES:]
    for _ in range(2):
        inv = inv + three(inv, eye - exact(mat, inv))
    return inv / bound


def by_distance(steps, far):
    return sorted(steps, key=lambda r: -far(r))


def kernel(
    nf, nd, tokens_all,
    attn_hbm, cot_hbm, kw_hbm, pin_hbm, pout_hbm, query_hbm, owner_hbm, ids_hbm,
    out_ref,
    attn, cot, kw, pin_ref, pout_ref, query_ref, owner_ref, ids_ref, part, cross, joint, rs_buf, chunks, gram_part, ga_buf, gs_buf, gb_own, gb_buf, gfull, qall, select, flat, stage,
    load_sem, *sems,
):
    (
        rs_sems, cross_sems, ag_sems, far_sems, hand_sems, ga_sems, gs_sems, gb_sems, gc_sems,
        x_sems, q_sems, p_sems, q2_sems, p2_sems, sib_sems,
    ) = zip(sems[::2], sems[1::2])
    f = lax.axis_index("fsdp")
    j = lax.axis_index("dp")
    ntb = nf // 2
    nch = nd // 2
    rows = R // ntb
    core, chip = lax.rem(j, 2), j // 2
    side, block = lax.rem(f, 2), f // 2
    half = query_ref.shape[2] // 2
    per = query_ref.shape[1]

    load_attn = pltpu.make_async_copy(attn_hbm, attn, load_sem.at[0])
    load_pin = pltpu.make_async_copy(pin_hbm, pin_ref, load_sem.at[1])
    load_kw = pltpu.make_async_copy(kw_hbm, kw, load_sem.at[2])
    load_pout = pltpu.make_async_copy(pout_hbm, pout_ref, load_sem.at[3])
    load_cot = pltpu.make_async_copy(cot_hbm, cot, load_sem.at[4])
    load_query = pltpu.make_async_copy(query_hbm, query_ref, load_sem.at[5])
    load_owner = pltpu.make_async_copy(owner_hbm, owner_ref, load_sem.at[6])
    load_ids = pltpu.make_async_copy(ids_hbm, ids_ref, load_sem.at[7])
    for load in (load_attn, load_pin, load_kw, load_pout, load_cot, load_query, load_owner, load_ids):
        load.start()

    ny, nz = nf // 2, nd // 4
    f_far = lambda r: min(r % ny, ny - r % ny) + (r >= ny)
    z_far = lambda r: min(r % nz, nz - r % nz) + 2 * (r >= nz)
    f_steps = by_distance(range(1, nf), f_far)
    d_steps = by_distance(range(1, nch), z_far)
    sibling = {"dp": j + 1 - 2 * core}
    over_f = lambda r: {"fsdp": lax.rem(f + r, nf)}
    over_d = lambda r: {"dp": lax.rem(j + 2 * r, nd)}

    barrier = pltpu.get_barrier_semaphore()
    for peer in [over_d(r) for r in d_steps] + [over_f(r) for r in f_steps] + [sibling]:
        pl.semaphore_signal(barrier, inc=1, device_id=peer, device_id_type=MESH)

    def send(src, dst, sems, peer):
        copy = pltpu.make_async_remote_copy(
            src_ref=src, dst_ref=dst, send_sem=sems[0], recv_sem=sems[1], device_id=peer, device_id_type=MESH
        )
        copy.start()
        return copy

    load_attn.wait()
    load_pin.wait()
    u_part = bf_dot(pin_ref[...], attn[...], NT)
    for t in range(ntb):
        part[2 * t] = u_part[:, LANES * t:LANES * (t + 1)]

    load_kw.wait()
    load_pout.wait()
    w_part = bf_dot(pout_ref[...], kw[...])
    w_two = jnp.concatenate(halves(w_part), axis=0)
    load_cot.wait()
    v_two = bf_dot(w_two, cot[...], NT)
    v_part = v_two[:R] + v_two[R:]
    for t in range(ntb):
        part[2 * t + 1] = v_part[:, LANES * t:LANES * (t + 1)]
    pl.semaphore_wait(barrier, nf - 1 + nch)

    col, y = f // ny, lax.rem(f, ny)
    place_of = lambda c, d: c * ny + lax.rem(y + d, ny)
    near, far = split_ring(ny)
    other = 1 - col
    pair_f = {"fsdp": place_of(other, 0)}
    for k, d in enumerate(far):
        send(part.at[place_of(other, d)], cross.at[k], cross_sems, pair_f)
    for k, d in enumerate(near):
        for i, c in enumerate((other, col)):
            to = place_of(c, d)
            send(part.at[to], rs_buf.at[1 + 2 * k + i], rs_sems, {"fsdp": to})
    send(part.at[place_of(other, 0)], rs_buf.at[0], rs_sems, pair_f)

    load_query.wait()
    own_q = query_ref[0]
    z, x = lax.rem(chip, nz), chip // nz
    partner = 1 - x
    qall[core, z, x] = jnp.concatenate([own_q[:, :half], own_q[:, half:]], axis=0)
    across = send(qall.at[core, z, x], qall.at[core, z, x], x_sems, {"dp": lax.rem(j + nch, nd)})
    z_near, z_rest = split_ring(nz)

    def hand(origin, c, d, pair_sems):
        block = qall.at[core, lax.rem(z + origin, nz), c]
        send(block, block, pair_sems, {"dp": (x * nz + lax.rem(z + d, nz)) * 2 + core})

    def await_blocks(count, sem):
        if count:
            some = qall.at[0, pl.ds(0, count), 0]
            pltpu.make_async_copy(some, some, sem).wait()

    def onward(c, near_sems, rest_sems):
        await_blocks(len(z_near), near_sems[1])
        if z_rest:
            hand(nz - 2, c, 2, rest_sems)
            hand(nz - 2, c, 1, rest_sems)
            hand(2, c, nz - 1, rest_sems)

    for d in z_near:
        hand(0, x, d, q_sems)

    if far:
        pltpu.make_async_copy(cross, cross, cross_sems[1]).wait()
    for k, d in enumerate(far):
        to = place_of(col, d)
        joint[k] = part[to] + cross[k]
        send(joint.at[k], rs_buf.at[1 + 2 * len(near) + k], rs_sems, {"fsdp": to})

    load_owner.wait()
    owner = jnp.concatenate([owner_ref[...]] * per, axis=1)
    cols = lax.broadcasted_iota(jnp.int32, select.shape, 1)
    rws = lax.broadcasted_iota(jnp.int32, select.shape, 0)
    block_of = rws // (2 * per)
    holder = (lax.rem(block_of, 2) * nz + lax.rem(block_of // 2, nz)) * 2 + block_of // nch
    hit = jnp.logical_and(holder == owner, lax.rem(rws, per) == cols // nd)
    select[...] = hit.astype(F32).astype(BF16)

    across.wait_recv()
    for d in z_near:
        hand(0, partner, d, p_sems)
    onward(x, q_sems, q2_sems)
    onward(partner, p_sems, p2_sems)

    row_id = lax.broadcasted_iota(jnp.int32, (LANES, LANES), 0)
    col_id = lax.broadcasted_iota(jnp.int32, (LANES, LANES), 1)
    eye = (row_id == col_id).astype(F32)
    left_half = lax.broadcasted_iota(jnp.int32, (1, LANES), 1) < R

    pltpu.make_async_copy(rs_buf, rs_buf, rs_sems[1]).wait()
    mine = part[f]
    for r in range(rs_buf.shape[0]):
        mine = mine + rs_buf[r]
    chunks[f] = mine

    zero = jnp.zeros_like(mine)
    wide = jnp.concatenate([jnp.where(side == 0, mine, zero), jnp.where(side == 0, zero, mine)], axis=0)
    gram = exact(mine, wide, NT)
    for t in range(ntb):
        gram_part[t] = gram[rows * t:rows * (t + 1)]

    for r in by_distance(range(1, ntb), lambda r: f_far(2 * r)):
        to = lax.rem(block + r, ntb)
        send(gram_part.at[to], ga_buf.at[r - 1], ga_sems, {"fsdp": 2 * to + side})
    for d in far:
        send(chunks.at[f], chunks.at[f], far_sems, {"fsdp": place_of(col, d)})
    for d in near:
        for c in (other, col):
            send(chunks.at[f], chunks.at[f], ag_sems, {"fsdp": place_of(c, d)})
    send(chunks.at[f], chunks.at[f], ag_sems, pair_f)

    pltpu.make_async_copy(ga_buf, ga_buf, ga_sems[1]).wait()
    gsum = gram_part[block]
    for r in range(ntb - 1):
        gsum = gsum + ga_buf[r]
    gb_own[0] = gsum
    twin = send(gb_own.at[0], gs_buf, gs_sems, sibling)
    twin.wait_recv()
    gsum = gsum + gs_buf[...]
    gb_own[1] = gsum
    for r in d_steps:
        send(gb_own.at[1], gb_buf.at[r - 1], gb_sems, over_d(r))
    far_chunks = chunks.at[pl.ds(0, len(far))]
    if far:
        pltpu.make_async_copy(far_chunks, far_chunks, far_sems[1]).wait()
    for d in far:
        held = chunks.at[place_of(col, d)]
        send(held, held, hand_sems, pair_f)

    pltpu.make_async_copy(gb_buf, gb_buf, gb_sems[1]).wait()
    for r in range(nch - 1):
        gsum = gsum + gb_buf[r]
    place = side * ntb + block
    gfull[place] = gsum

    for r in f_steps:
        send(gfull.at[place], gfull.at[place], gc_sems, over_f(r))

    await_blocks(len(z_rest), q2_sems[1])
    await_blocks(len(z_rest), p2_sems[1])
    twin_q = send(qall.at[core], qall.at[core], sib_sems, sibling)

    near_chunks = chunks.at[pl.ds(0, 1 + 2 * len(near))]
    pltpu.make_async_copy(near_chunks, near_chunks, ag_sems[1]).wait()
    if far:
        pltpu.make_async_copy(far_chunks, far_chunks, hand_sems[1]).wait()
    u_high, u_low = halves(jnp.concatenate([chunks[2 * t] for t in range(ntb)], axis=1))
    v_high, v_low = halves(jnp.concatenate([chunks[2 * t + 1] for t in range(ntb)], axis=1))
    v_both = jnp.concatenate([v_high, v_low], axis=0)
    load_ids.wait()
    ids = ids_ref[...]
    none = jnp.zeros_like(u_high)
    pair = EX // 2
    for p in range(pair):
        marks = [jnp.broadcast_to(ids == e, u_high.shape) for e in (p, p + pair)]
        masked_high = jnp.concatenate([jnp.where(m, u_high, none) for m in marks], axis=0)
        masked_low = jnp.concatenate([jnp.where(m, u_low, none) for m in marks], axis=0)
        top = bf_dot(v_both, masked_high, NT)
        stage[pl.ds(R * p, R), :] = top[:R] + top[R:] + bf_dot(v_high, masked_low, NT)

    all_grams = gfull.at[pl.ds(0, nf - 1)]
    pltpu.make_async_copy(all_grams, all_grams, gc_sems[1]).wait()
    inv = inverse_pair(jnp.concatenate([gfull[t] for t in range(nf)], axis=0), eye, left_half, 1.0 / tokens_all)
    corner = jnp.where(jnp.logical_and(row_id < R, col_id < R), inv, 0.0)
    twice = corner + pltpu.roll(pltpu.roll(corner, R, 0), R, 1)
    right = three(stage[...], twice)
    right = jnp.concatenate([right[R * p:R * (p + 1)] for p in range(pair)], axis=1)
    both = three(inv[R:], jnp.concatenate([right, right], axis=0))
    for p in range(pair):
        stage[pl.ds(R * p, R), :] = both[:, LANES * p:LANES * (p + 1)]
    for i in range(R // 2):
        a = stage[pl.ds(2 * i, pair, stride=R), :]
        b = stage[pl.ds(2 * i + 1, pair, stride=R), :]
        low = jnp.where(left_half, a, pltpu.roll(b, R, 1))
        high = jnp.where(left_half, pltpu.roll(a, R, 1), b)
        big, small = halves(jnp.concatenate([low, high], axis=0))
        top, left = (2 * i * R) // half * 2 * EX, (2 * i * R) % half
        flat[pl.ds(top, EX), pl.ds(left, LANES)] = big
        flat[pl.ds(top + EX, EX), pl.ds(left, LANES)] = small

    twin_q.wait_recv()
    raw = bf_dot(flat[...], qall[...].reshape(nd * 2 * per, half), NT)
    first = raw[:EX] + raw[EX:2 * EX]
    second = raw[2 * EX:3 * EX] + raw[3 * EX:]
    column = lax.broadcasted_iota(jnp.int32, first.shape, 1)
    sums = jnp.where(lax.rem(column // per, 2) == 0, first, second)
    big = sums.astype(BF16)
    rest = sums - big.astype(F32)
    mid = rest.astype(BF16)
    tail = (rest - mid.astype(F32)).astype(BF16)
    picked = bf_dot(jnp.concatenate([big, mid, tail], axis=0), select[...])
    picked = (picked[:EX] + picked[EX:2 * EX] + picked[2 * EX:]) * (1.0 / (R * R))
    for i in range(per):
        out_ref[:, i, :] = picked[:, nd * i:nd * (i + 1)]

    across.wait_send()
    twin.wait_send()
    twin_q.wait_send()
    for buf, pair_sems in (
        (rs_buf, rs_sems), (near_chunks, ag_sems), (ga_buf, ga_sems), (gb_buf, gb_sems), (all_grams, gc_sems),
    ):
        pltpu.make_async_copy(buf, buf, pair_sems[0]).wait()
    if far:
        pltpu.make_async_copy(cross, cross, cross_sems[0]).wait()
        pltpu.make_async_copy(far_chunks, far_chunks, far_sems[0]).wait()
        pltpu.make_async_copy(far_chunks, far_chunks, hand_sems[0]).wait()
    for count, pair_sems in ((z_near, q_sems), (z_near, p_sems), (z_rest, q2_sems), (z_rest, p2_sems)):
        await_blocks(len(count), pair_sems[0])


def on_device(
    nf, nd, attn_out, key_cotangent, key_weight, proj_in, proj_out, query_sketches, block_owner, example_ids
):
    tokens = attn_out.shape[0]
    per = query_sketches.shape[1]
    half = query_sketches.shape[2] // 2
    ntb = nf // 2
    rows = R // ntb
    far = len(split_ring(ntb)[1])
    hbm = pl.BlockSpec(memory_space=pl.ANY)
    vmem = pl.BlockSpec(memory_space=pltpu.VMEM)
    scores = pl.pallas_call(
        functools.partial(kernel, nf, nd, nd * tokens),
        out_shape=jax.ShapeDtypeStruct((EX, per, nd), F32),
        in_specs=[hbm] * 8,
        out_specs=vmem,
        scratch_shapes=[
            pltpu.VMEM(attn_out.shape, BF16),
            pltpu.VMEM(key_cotangent.shape, BF16),
            pltpu.VMEM(key_weight.shape, BF16),
            pltpu.VMEM(proj_in.shape, BF16),
            pltpu.VMEM(proj_out.shape, BF16),
            pltpu.VMEM(query_sketches.shape, BF16),
            pltpu.VMEM((1, nd), jnp.int32),
            pltpu.VMEM(example_ids.shape, jnp.int32),
            pltpu.VMEM((nf, R, LANES), F32),
            pltpu.VMEM((max(1, far), R, LANES), F32),
            pltpu.VMEM((max(1, far), R, LANES), F32),
            pltpu.VMEM((nf - 1 - far, R, LANES), F32),
            pltpu.VMEM((nf, R, LANES), F32),
            pltpu.VMEM((ntb, rows, LANES), F32),
            pltpu.VMEM((ntb - 1, rows, LANES), F32),
            pltpu.VMEM((rows, LANES), F32),
            pltpu.VMEM((2, rows, LANES), F32),
            pltpu.VMEM((nd // 2 - 1, rows, LANES), F32),
            pltpu.VMEM((nf, rows, LANES), F32),
            pltpu.VMEM((2, nd // 4, 2, 2 * per, half), BF16),
            pltpu.VMEM((nd * 2 * per, per * nd), BF16),
            pltpu.VMEM((4 * EX, half), BF16),
            pltpu.VMEM((EX // 2 * R, LANES), F32),
            pltpu.SemaphoreType.DMA((8,)),
        ] + [pltpu.SemaphoreType.DMA] * 30,
        compiler_params=pltpu.CompilerParams(
            collective_id=0, has_side_effects=True, vmem_limit_bytes=62 * 1024 * 1024
        ),
        name="influence",
    )(
        attn_out, key_cotangent, key_weight, proj_in, proj_out, query_sketches,
        block_owner.reshape(1, nd), example_ids,
    )
    return scores.transpose(0, 2, 1)


def solution(mesh):
    return jax.shard_map(
        functools.partial(on_device, mesh.shape["fsdp"], mesh.shape["dp"]),
        mesh=mesh,
        in_specs=(
            P("dp", "fsdp"),
            P("dp", None),
            P("fsdp", None),
            P(None, "fsdp"),
            P(None, "fsdp"),
            P("dp", "fsdp", None),
            P(),
            P("dp", None),
        ),
        out_specs=P("dp", None, "fsdp"),
        check_vma=False,
    )
```

```python
import functools
import jax
import jax.numpy as jnp
from jax import lax
from jax.experimental import pallas as pl
from jax.experimental.pallas import tpu as pltpu
from jax.sharding import PartitionSpec as P

EX = 16
R = 64
LANES = 128
MESH = pl.DeviceIdType.MESH
NT = (((1,), (1,)), ((), ()))
F32 = jnp.float32
BF16 = jnp.bfloat16


def exact(a, b, dims=(((1,), (0,)), ((), ()))):
    return lax.dot_general(a, b, dims, precision=lax.Precision.HIGHEST, preferred_element_type=F32)


def bf_dot(a, b, dims=(((1,), (0,)), ((), ()))):
    return lax.dot_general(a, b, dims, preferred_element_type=F32)


def halves(x):
    high = x.astype(BF16)
    return high, (x - high.astype(F32)).astype(BF16)


def three(a, b):
    a_high, a_low = halves(a)
    b_high, b_low = halves(b)
    return bf_dot(jnp.concatenate([a_high, a_low, a_high], axis=1), jnp.concatenate([b_high, b_high, b_low], axis=0))


def split_ring(n):
    near = [d for d in (n - 2, 2, n - 1, 1) if 0 < d < n]
    near = sorted(set(near), key=near.index)
    return near, [d for d in (n // 2, n // 2 - 1, n // 2 + 1) if 0 < d < n and d not in near]


def inverse_pair(gram, eye, left_half, scale):
    diag = jnp.sum(gram * eye, axis=0, keepdims=True) * scale
    tr_in = jnp.sum(jnp.where(left_half, diag, 0.0), axis=1, keepdims=True)
    tr_out = jnp.sum(jnp.where(left_half, 0.0, diag), axis=1, keepdims=True)
    bound = jnp.where(left_half, tr_in, tr_out) * (1.0 + 0.1 / R)
    low = (0.1 / R) / (1.0 + 0.1 / R)
    mat = gram * (scale / bound) + low * eye
    start = 2.0 / (1.0 + low)
    rho = (1.0 - low) / (1.0 + low)
    gain = 2.0 / (2.0 - rho * rho)
    rho = rho * rho / (2.0 - rho * rho)
    prod = start * mat
    turn = 2.0 * eye - prod
    inv = (gain * start) * turn
    prod = gain * three(prod, turn)
    while rho > 0.05:
        gain = 2.0 / (2.0 - rho * rho)
        rho = rho * rho / (2.0 - rho * rho)
        turn = 2.0 * eye - prod
        both = three(jnp.concatenate([prod, inv], axis=0), turn) * gain
        prod, inv = both[:LANES], both[LANES:]
    for _ in range(2):
        inv = inv + three(inv, eye - exact(mat, inv))
    return inv / bound


def by_distance(steps, far):
    return sorted(steps, key=lambda r: -far(r))


def kernel(
    nf, nd, tokens_all,
    attn_hbm, cot_hbm, kw_hbm, pin_hbm, pout_hbm, query_hbm, owner_hbm, ids_hbm,
    out_ref,
    attn, cot, kw, pin_ref, pout_ref, query_ref, owner_ref, ids_ref, part, cross, joint, rs_buf, chunks, gram_part, ga_buf, gs_buf, gb_own, gb_buf, gfull, qall, select, flat, stage,
    load_sem, relay, *sems,
):
    (
        rs_sems, cross_sems, ag_sems, far_sems, hand_sems, ga_sems, gs_sems, gb_sems, gc_sems,
        x_sems, q_sems, p_sems, q2_sems, p2_sems, sib_sems,
    ) = zip(sems[::2], sems[1::2])
    f = lax.axis_index("fsdp")
    j = lax.axis_index("dp")
    ntb = nf // 2
    nch = nd // 2
    rows = R // ntb
    core, chip = lax.rem(j, 2), j // 2
    side, block = lax.rem(f, 2), f // 2
    half = query_ref.shape[2] // 2
    per = query_ref.shape[1]

    load_attn = pltpu.make_async_copy(attn_hbm, attn, load_sem.at[0])
    load_pin = pltpu.make_async_copy(pin_hbm, pin_ref, load_sem.at[1])
    load_kw = pltpu.make_async_copy(kw_hbm, kw, load_sem.at[2])
    load_pout = pltpu.make_async_copy(pout_hbm, pout_ref, load_sem.at[3])
    load_cot = pltpu.make_async_copy(cot_hbm, cot, load_sem.at[4])
    load_query = pltpu.make_async_copy(query_hbm, query_ref, load_sem.at[5])
    load_owner = pltpu.make_async_copy(owner_hbm, owner_ref, load_sem.at[6])
    load_ids = pltpu.make_async_copy(ids_hbm, ids_ref, load_sem.at[7])
    for load in (load_attn, load_pin, load_kw, load_pout, load_cot, load_query, load_owner, load_ids):
        load.start()

    ny, nz = nf // 2, nd // 4
    f_far = lambda r: min(r % ny, ny - r % ny) + (r >= ny)
    z_far = lambda r: min(r % nz, nz - r % nz) + 2 * (r >= nz)
    f_steps = by_distance(range(1, nf), f_far)
    d_steps = by_distance(range(1, nch), z_far)
    sibling = {"dp": j + 1 - 2 * core}
    over_f = lambda r: {"fsdp": lax.rem(f + r, nf)}
    over_d = lambda r: {"dp": lax.rem(j + 2 * r, nd)}

    col, y = f // ny, lax.rem(f, ny)
    place_of = lambda c, d: c * ny + lax.rem(y + d, ny)
    near, far = split_ring(ny)
    other = 1 - col
    pair_f = {"fsdp": place_of(other, 0)}
    z, x = lax.rem(chip, nz), chip // nz
    partner = 1 - x
    z_near, z_rest = split_ring(nz)
    over_z = lambda d: {"dp": (x * nz + lax.rem(z + d, nz)) * 2 + core}
    pair_d = {"dp": lax.rem(j + nch, nd)}
    greeted = [pair_f, pair_d, sibling] + [over_z(d) for d in z_near]
    greeted += [{"fsdp": place_of(c, d)} for d in near for c in (other, col)]
    barrier = pltpu.get_barrier_semaphore()
    for peer in reversed(greeted):
        pl.semaphore_signal(barrier, inc=1, device_id=peer, device_id_type=MESH)

    def send(src, dst, sems, peer):
        copy = pltpu.make_async_remote_copy(
            src_ref=src, dst_ref=dst, send_sem=sems[0], recv_sem=sems[1], device_id=peer, device_id_type=MESH
        )
        copy.start()
        return copy

    load_attn.wait()
    load_pin.wait()
    u_part = bf_dot(pin_ref[...], attn[...], NT)
    for t in range(ntb):
        part[2 * t] = u_part[:, LANES * t:LANES * (t + 1)]

    load_kw.wait()
    load_pout.wait()
    w_part = bf_dot(pout_ref[...], kw[...])
    w_two = jnp.concatenate(halves(w_part), axis=0)
    load_cot.wait()
    v_two = bf_dot(w_two, cot[...], NT)
    v_part = v_two[:R] + v_two[R:]
    for t in range(ntb):
        part[2 * t + 1] = v_part[:, LANES * t:LANES * (t + 1)]
    pl.semaphore_wait(barrier, len(greeted))
    relays = [2, ny - 2] if far else []
    for d in relays:
        pl.semaphore_signal(relay, inc=1, device_id={"fsdp": place_of(col, d)}, device_id_type=MESH)

    for k, d in enumerate(far):
        send(part.at[place_of(other, d)], cross.at[k], cross_sems, pair_f)
    for k, d in enumerate(near):
        for i, c in enumerate((other, col)):
            to = place_of(c, d)
            send(part.at[to], rs_buf.at[1 + 2 * k + i], rs_sems, {"fsdp": to})
    send(part.at[place_of(other, 0)], rs_buf.at[0], rs_sems, pair_f)

    load_query.wait()
    own_q = query_ref[0]
    qall[core, z, x] = jnp.concatenate([own_q[:, :half], own_q[:, half:]], axis=0)
    across = send(qall.at[core, z, x], qall.at[core, z, x], x_sems, pair_d)

    def hand(origin, c, d, pair_sems):
        block = qall.at[core, lax.rem(z + origin, nz), c]
        send(block, block, pair_sems, over_z(d))

    def await_blocks(count, sem):
        if count:
            some = qall.at[0, pl.ds(0, count), 0]
            pltpu.make_async_copy(some, some, sem).wait()

    def onward(c, near_sems, rest_sems):
        await_blocks(len(z_near), near_sems[1])
        if z_rest:
            hand(nz - 2, c, 2, rest_sems)
            hand(nz - 2, c, 1, rest_sems)
            hand(2, c, nz - 1, rest_sems)

    for d in z_near:
        hand(0, x, d, q_sems)

    if far:
        pl.semaphore_wait(relay, len(relays))
        pltpu.make_async_copy(cross, cross, cross_sems[1]).wait()
    for k, d in enumerate(far):
        to = place_of(col, d)
        joint[k] = part[to] + cross[k]
        send(joint.at[k], rs_buf.at[1 + 2 * len(near) + k], rs_sems, {"fsdp": to})

    load_owner.wait()
    owner = jnp.concatenate([owner_ref[...]] * per, axis=1)
    cols = lax.broadcasted_iota(jnp.int32, select.shape, 1)
    rws = lax.broadcasted_iota(jnp.int32, select.shape, 0)
    block_of = rws // (2 * per)
    holder = (lax.rem(block_of, 2) * nz + lax.rem(block_of // 2, nz)) * 2 + block_of // nch
    hit = jnp.logical_and(holder == owner, lax.rem(rws, per) == cols // nd)
    select[...] = hit.astype(F32).astype(BF16)

    across.wait_recv()
    for d in z_near:
        hand(0, partner, d, p_sems)
    onward(x, q_sems, q2_sems)

    row_id = lax.broadcasted_iota(jnp.int32, (LANES, LANES), 0)
    col_id = lax.broadcasted_iota(jnp.int32, (LANES, LANES), 1)
    eye = (row_id == col_id).astype(F32)
    left_half = lax.broadcasted_iota(jnp.int32, (1, LANES), 1) < R

    pltpu.make_async_copy(rs_buf, rs_buf, rs_sems[1]).wait()
    mine = part[f]
    for r in range(rs_buf.shape[0]):
        mine = mine + rs_buf[r]
    chunks[f] = mine

    zero = jnp.zeros_like(mine)
    wide = jnp.concatenate([jnp.where(side == 0, mine, zero), jnp.where(side == 0, zero, mine)], axis=0)
    gram = exact(mine, wide, NT)
    for t in range(ntb):
        gram_part[t] = gram[rows * t:rows * (t + 1)]

    for r in by_distance(range(1, ntb), lambda r: f_far(2 * r)):
        to = lax.rem(block + r, ntb)
        send(gram_part.at[to], ga_buf.at[r - 1], ga_sems, {"fsdp": 2 * to + side})
    for d in far:
        send(chunks.at[f], chunks.at[f], far_sems, {"fsdp": place_of(col, d)})
    for d in near:
        for c in (other, col):
            send(chunks.at[f], chunks.at[f], ag_sems, {"fsdp": place_of(c, d)})
    send(chunks.at[f], chunks.at[f], ag_sems, pair_f)

    onward(partner, p_sems, p2_sems)
    pltpu.make_async_copy(ga_buf, ga_buf, ga_sems[1]).wait()
    gsum = gram_part[block]
    for r in range(ntb - 1):
        gsum = gsum + ga_buf[r]
    gb_own[0] = gsum
    twin = send(gb_own.at[0], gs_buf, gs_sems, sibling)
    twin.wait_recv()
    gsum = gsum + gs_buf[...]
    gb_own[1] = gsum
    for r in d_steps:
        send(gb_own.at[1], gb_buf.at[r - 1], gb_sems, over_d(r))
    far_chunks = chunks.at[pl.ds(0, len(far))]
    if far:
        pltpu.make_async_copy(far_chunks, far_chunks, far_sems[1]).wait()
    for d in far:
        held = chunks.at[place_of(col, d)]
        send(held, held, hand_sems, pair_f)

    pltpu.make_async_copy(gb_buf, gb_buf, gb_sems[1]).wait()
    for r in range(nch - 1):
        gsum = gsum + gb_buf[r]
    place = side * ntb + block
    gfull[place] = gsum

    for r in f_steps:
        send(gfull.at[place], gfull.at[place], gc_sems, over_f(r))

    await_blocks(len(z_rest), q2_sems[1])
    await_blocks(len(z_rest), p2_sems[1])
    twin_q = send(qall.at[core], qall.at[core], sib_sems, sibling)

    near_chunks = chunks.at[pl.ds(0, 1 + 2 * len(near))]
    pltpu.make_async_copy(near_chunks, near_chunks, ag_sems[1]).wait()
    if far:
        pltpu.make_async_copy(far_chunks, far_chunks, hand_sems[1]).wait()
    u_high, u_low = halves(jnp.concatenate([chunks[2 * t] for t in range(ntb)], axis=1))
    v_high, v_low = halves(jnp.concatenate([chunks[2 * t + 1] for t in range(ntb)], axis=1))
    v_both = jnp.concatenate([v_high, v_low], axis=0)
    load_ids.wait()
    ids = ids_ref[...]
    none = jnp.zeros_like(u_high)
    pair = EX // 2
    for p in range(pair):
        marks = [jnp.broadcast_to(ids == e, u_high.shape) for e in (p, p + pair)]
        masked_high = jnp.concatenate([jnp.where(m, u_high, none) for m in marks], axis=0)
        masked_low = jnp.concatenate([jnp.where(m, u_low, none) for m in marks], axis=0)
        top = bf_dot(v_both, masked_high, NT)
        stage[pl.ds(R * p, R), :] = top[:R] + top[R:] + bf_dot(v_high, masked_low, NT)

    all_grams = gfull.at[pl.ds(0, nf - 1)]
    pltpu.make_async_copy(all_grams, all_grams, gc_sems[1]).wait()
    inv = inverse_pair(jnp.concatenate([gfull[t] for t in range(nf)], axis=0), eye, left_half, 1.0 / tokens_all)
    corner = jnp.where(jnp.logical_and(row_id < R, col_id < R), inv, 0.0)
    twice = corner + pltpu.roll(pltpu.roll(corner, R, 0), R, 1)
    right = three(stage[...], twice)
    right = jnp.concatenate([right[R * p:R * (p + 1)] for p in range(pair)], axis=1)
    both = three(inv[R:], jnp.concatenate([right, right], axis=0))
    for p in range(pair):
        stage[pl.ds(R * p, R), :] = both[:, LANES * p:LANES * (p + 1)]
    for i in range(R // 2):
        a = stage[pl.ds(2 * i, pair, stride=R), :]
        b = stage[pl.ds(2 * i + 1, pair, stride=R), :]
        low = jnp.where(left_half, a, pltpu.roll(b, R, 1))
        high = jnp.where(left_half, pltpu.roll(a, R, 1), b)
        big, small = halves(jnp.concatenate([low, high], axis=0))
        top, left = (2 * i * R) // half * 2 * EX, (2 * i * R) % half
        flat[pl.ds(top, EX), pl.ds(left, LANES)] = big
        flat[pl.ds(top + EX, EX), pl.ds(left, LANES)] = small

    twin_q.wait_recv()
    raw = bf_dot(flat[...], qall[...].reshape(nd * 2 * per, half), NT)
    first = raw[:EX] + raw[EX:2 * EX]
    second = raw[2 * EX:3 * EX] + raw[3 * EX:]
    column = lax.broadcasted_iota(jnp.int32, first.shape, 1)
    sums = jnp.where(lax.rem(column // per, 2) == 0, first, second)
    big = sums.astype(BF16)
    rest = sums - big.astype(F32)
    mid = rest.astype(BF16)
    tail = (rest - mid.astype(F32)).astype(BF16)
    picked = bf_dot(jnp.concatenate([big, mid, tail], axis=0), select[...])
    picked = (picked[:EX] + picked[EX:2 * EX] + picked[2 * EX:]) * (1.0 / (R * R))
    for i in range(per):
        out_ref[:, i, :] = picked[:, nd * i:nd * (i + 1)]

    across.wait_send()
    twin.wait_send()
    twin_q.wait_send()
    for buf, pair_sems in (
        (rs_buf, rs_sems), (near_chunks, ag_sems), (ga_buf, ga_sems), (gb_buf, gb_sems), (all_grams, gc_sems),
    ):
        pltpu.make_async_copy(buf, buf, pair_sems[0]).wait()
    if far:
        pltpu.make_async_copy(cross, cross, cross_sems[0]).wait()
        pltpu.make_async_copy(far_chunks, far_chunks, far_sems[0]).wait()
        pltpu.make_async_copy(far_chunks, far_chunks, hand_sems[0]).wait()
    for count, pair_sems in ((z_near, q_sems), (z_near, p_sems), (z_rest, q2_sems), (z_rest, p2_sems)):
        await_blocks(len(count), pair_sems[0])


def on_device(
    nf, nd, attn_out, key_cotangent, key_weight, proj_in, proj_out, query_sketches, block_owner, example_ids
):
    tokens = attn_out.shape[0]
    per = query_sketches.shape[1]
    half = query_sketches.shape[2] // 2
    ntb = nf // 2
    rows = R // ntb
    far = len(split_ring(ntb)[1])
    hbm = pl.BlockSpec(memory_space=pl.ANY)
    vmem = pl.BlockSpec(memory_space=pltpu.VMEM)
    scores = pl.pallas_call(
        functools.partial(kernel, nf, nd, nd * tokens),
        out_shape=jax.ShapeDtypeStruct((EX, per, nd), F32),
        in_specs=[hbm] * 8,
        out_specs=vmem,
        scratch_shapes=[
            pltpu.VMEM(attn_out.shape, BF16),
            pltpu.VMEM(key_cotangent.shape, BF16),
            pltpu.VMEM(key_weight.shape, BF16),
            pltpu.VMEM(proj_in.shape, BF16),
            pltpu.VMEM(proj_out.shape, BF16),
            pltpu.VMEM(query_sketches.shape, BF16),
            pltpu.VMEM((1, nd), jnp.int32),
            pltpu.VMEM(example_ids.shape, jnp.int32),
            pltpu.VMEM((nf, R, LANES), F32),
            pltpu.VMEM((max(1, far), R, LANES), F32),
            pltpu.VMEM((max(1, far), R, LANES), F32),
            pltpu.VMEM((nf - 1 - far, R, LANES), F32),
            pltpu.VMEM((nf, R, LANES), F32),
            pltpu.VMEM((ntb, rows, LANES), F32),
            pltpu.VMEM((ntb - 1, rows, LANES), F32),
            pltpu.VMEM((rows, LANES), F32),
            pltpu.VMEM((2, rows, LANES), F32),
            pltpu.VMEM((nd // 2 - 1, rows, LANES), F32),
            pltpu.VMEM((nf, rows, LANES), F32),
            pltpu.VMEM((2, nd // 4, 2, 2 * per, half), BF16),
            pltpu.VMEM((nd * 2 * per, per * nd), BF16),
            pltpu.VMEM((4 * EX, half), BF16),
            pltpu.VMEM((EX // 2 * R, LANES), F32),
            pltpu.SemaphoreType.DMA((8,)),
            pltpu.SemaphoreType.REGULAR,
        ] + [pltpu.SemaphoreType.DMA] * 30,
        compiler_params=pltpu.CompilerParams(
            collective_id=0, has_side_effects=True, vmem_limit_bytes=62 * 1024 * 1024
        ),
        name="influence",
    )(
        attn_out, key_cotangent, key_weight, proj_in, proj_out, query_sketches,
        block_owner.reshape(1, nd), example_ids,
    )
    return scores.transpose(0, 2, 1)


def solution(mesh):
    return jax.shard_map(
        functools.partial(on_device, mesh.shape["fsdp"], mesh.shape["dp"]),
        mesh=mesh,
        in_specs=(
            P("dp", "fsdp"),
            P("dp", None),
            P("fsdp", None),
            P(None, "fsdp"),
            P(None, "fsdp"),
            P("dp", "fsdp", None),
            P(),
            P("dp", None),
        ),
        out_specs=P("dp", None, "fsdp"),
        check_vma=False,
    )
```

```python
import functools
import jax
import jax.numpy as jnp
from jax import lax
from jax.experimental import pallas as pl
from jax.experimental.pallas import tpu as pltpu
from jax.sharding import PartitionSpec as P

EX = 16
R = 64
LANES = 128
MESH = pl.DeviceIdType.MESH
NT = (((1,), (1,)), ((), ()))
F32 = jnp.float32
BF16 = jnp.bfloat16


def exact(a, b, dims=(((1,), (0,)), ((), ()))):
    return lax.dot_general(a, b, dims, precision=lax.Precision.HIGHEST, preferred_element_type=F32)


def bf_dot(a, b, dims=(((1,), (0,)), ((), ()))):
    return lax.dot_general(a, b, dims, preferred_element_type=F32)


def halves(x):
    high = x.astype(BF16)
    return high, (x - high.astype(F32)).astype(BF16)


def three(a, b):
    a_high, a_low = halves(a)
    b_high, b_low = halves(b)
    return bf_dot(jnp.concatenate([a_high, a_low, a_high], axis=1), jnp.concatenate([b_high, b_high, b_low], axis=0))


def split_ring(n):
    near = [d for d in (n - 2, 2, n - 1, 1) if 0 < d < n]
    near = sorted(set(near), key=near.index)
    return near, [d for d in (n // 2, n // 2 - 1, n // 2 + 1) if 0 < d < n and d not in near]


def inverse_pair(gram, eye, left_half, scale):
    diag = jnp.sum(gram * eye, axis=0, keepdims=True) * scale
    tr_in = jnp.sum(jnp.where(left_half, diag, 0.0), axis=1, keepdims=True)
    tr_out = jnp.sum(jnp.where(left_half, 0.0, diag), axis=1, keepdims=True)
    bound = jnp.where(left_half, tr_in, tr_out) * (1.0 + 0.1 / R)
    low = (0.1 / R) / (1.0 + 0.1 / R)
    mat = gram * (scale / bound) + low * eye
    start = 2.0 / (1.0 + low)
    rho = (1.0 - low) / (1.0 + low)
    gain = 2.0 / (2.0 - rho * rho)
    rho = rho * rho / (2.0 - rho * rho)
    prod = start * mat
    turn = 2.0 * eye - prod
    inv = (gain * start) * turn
    prod = gain * three(prod, turn)
    while rho > 0.05:
        gain = 2.0 / (2.0 - rho * rho)
        rho = rho * rho / (2.0 - rho * rho)
        turn = 2.0 * eye - prod
        both = three(jnp.concatenate([prod, inv], axis=0), turn) * gain
        prod, inv = both[:LANES], both[LANES:]
    for _ in range(2):
        inv = inv + three(inv, eye - exact(mat, inv))
    return inv / bound


def by_distance(steps, far):
    return sorted(steps, key=lambda r: -far(r))


def kernel(
    nf, nd, tokens_all,
    attn_hbm, cot_hbm, kw_hbm, pin_hbm, pout_hbm, query_hbm, owner_hbm, ids_hbm,
    out_ref,
    attn, cot, kw, pin_ref, pout_ref, query_ref, owner_ref, ids_ref, part, cross, joint, rs_buf, chunks, gram_part, ga_buf, gs_buf, gb_own, gb_buf, gfull, qall, select, flat, stage,
    load_sem, relay, *sems,
):
    (
        rs_sems, cross_sems, ag_sems, far_sems, hand_sems, ga_sems, gs_sems, gb_sems, gc_sems,
        x_sems, q_sems, p_sems, q2_sems, p2_sems, sib_sems,
    ) = zip(sems[::2], sems[1::2])
    f = lax.axis_index("fsdp")
    j = lax.axis_index("dp")
    ntb = nf // 2
    nch = nd // 2
    rows = R // ntb
    core, chip = lax.rem(j, 2), j // 2
    side, block = f // ntb, lax.rem(f, ntb)
    half = query_ref.shape[2] // 2
    per = query_ref.shape[1]

    load_attn = pltpu.make_async_copy(attn_hbm, attn, load_sem.at[0])
    load_pin = pltpu.make_async_copy(pin_hbm, pin_ref, load_sem.at[1])
    load_kw = pltpu.make_async_copy(kw_hbm, kw, load_sem.at[2])
    load_pout = pltpu.make_async_copy(pout_hbm, pout_ref, load_sem.at[3])
    load_cot = pltpu.make_async_copy(cot_hbm, cot, load_sem.at[4])
    load_query = pltpu.make_async_copy(query_hbm, query_ref, load_sem.at[5])
    load_owner = pltpu.make_async_copy(owner_hbm, owner_ref, load_sem.at[6])
    load_ids = pltpu.make_async_copy(ids_hbm, ids_ref, load_sem.at[7])
    for load in (load_attn, load_pin, load_kw, load_pout, load_cot, load_query, load_owner, load_ids):
        load.start()

    ny, nz = nf // 2, nd // 4
    f_far = lambda r: min(r % ny, ny - r % ny) + (r >= ny)
    z_far = lambda r: min(r % nz, nz - r % nz) + 2 * (r >= nz)
    f_steps = by_distance(range(1, nf), f_far)
    d_steps = by_distance(range(1, nch), z_far)
    sibling = {"dp": j + 1 - 2 * core}
    over_f = lambda r: {"fsdp": lax.rem(f + r, nf)}
    over_d = lambda r: {"dp": lax.rem(j + 2 * r, nd)}

    col, y = f // ny, lax.rem(f, ny)
    place_of = lambda c, d: c * ny + lax.rem(y + d, ny)
    near, far = split_ring(ny)
    other = 1 - col
    pair_f = {"fsdp": place_of(other, 0)}
    z, x = lax.rem(chip, nz), chip // nz
    partner = 1 - x
    z_near, z_rest = split_ring(nz)
    over_z = lambda d: {"dp": (x * nz + lax.rem(z + d, nz)) * 2 + core}
    pair_d = {"dp": lax.rem(j + nch, nd)}
    greeted = [pair_f, pair_d, sibling] + [over_z(d) for d in z_near]
    greeted += [{"fsdp": place_of(c, d)} for d in near for c in (other, col)]
    barrier = pltpu.get_barrier_semaphore()
    for peer in reversed(greeted):
        pl.semaphore_signal(barrier, inc=1, device_id=peer, device_id_type=MESH)

    def send(src, dst, sems, peer):
        copy = pltpu.make_async_remote_copy(
            src_ref=src, dst_ref=dst, send_sem=sems[0], recv_sem=sems[1], device_id=peer, device_id_type=MESH
        )
        copy.start()
        return copy

    load_attn.wait()
    load_pin.wait()
    u_part = bf_dot(pin_ref[...], attn[...], NT)
    for t in range(ntb):
        part[t] = u_part[:, LANES * t:LANES * (t + 1)]

    load_kw.wait()
    load_pout.wait()
    w_part = bf_dot(pout_ref[...], kw[...])
    w_two = jnp.concatenate(halves(w_part), axis=0)
    load_cot.wait()
    v_two = bf_dot(w_two, cot[...], NT)
    v_part = v_two[:R] + v_two[R:]
    for t in range(ntb):
        part[ntb + t] = v_part[:, LANES * t:LANES * (t + 1)]
    pl.semaphore_wait(barrier, len(greeted))
    relays = [2, ny - 2] if far else []
    for d in relays:
        pl.semaphore_signal(relay, inc=1, device_id={"fsdp": place_of(col, d)}, device_id_type=MESH)

    for k, d in enumerate(far):
        send(part.at[place_of(other, d)], cross.at[k], cross_sems, pair_f)
    for k, d in enumerate(near):
        for i, c in enumerate((other, col)):
            to = place_of(c, d)
            send(part.at[to], rs_buf.at[1 + 2 * k + i], rs_sems, {"fsdp": to})
    send(part.at[place_of(other, 0)], rs_buf.at[0], rs_sems, pair_f)

    load_query.wait()
    own_q = query_ref[0]
    qall[core, z, x] = jnp.concatenate([own_q[:, :half], own_q[:, half:]], axis=0)
    across = send(qall.at[core, z, x], qall.at[core, z, x], x_sems, pair_d)

    def hand(origin, c, d, pair_sems):
        block = qall.at[core, lax.rem(z + origin, nz), c]
        send(block, block, pair_sems, over_z(d))

    def await_blocks(count, sem):
        if count:
            some = qall.at[0, pl.ds(0, count), 0]
            pltpu.make_async_copy(some, some, sem).wait()

    def onward(c, rest_sems):
        if z_rest:
            hand(nz - 2, c, 2, rest_sems)
            hand(nz - 2, c, 1, rest_sems)
            hand(2, c, nz - 1, rest_sems)

    for d in z_near:
        hand(0, x, d, q_sems)

    if far:
        pl.semaphore_wait(relay, len(relays))
        pltpu.make_async_copy(cross, cross, cross_sems[1]).wait()
    for k, d in enumerate(far):
        to = place_of(col, d)
        joint[k] = part[to] + cross[k]
        send(joint.at[k], rs_buf.at[1 + 2 * len(near) + k], rs_sems, {"fsdp": to})

    load_owner.wait()
    owner = jnp.concatenate([owner_ref[...]] * per, axis=1)
    cols = lax.broadcasted_iota(jnp.int32, select.shape, 1)
    rws = lax.broadcasted_iota(jnp.int32, select.shape, 0)
    block_of = rws // (2 * per)
    holder = (lax.rem(block_of, 2) * nz + lax.rem(block_of // 2, nz)) * 2 + block_of // nch
    hit = jnp.logical_and(holder == owner, lax.rem(rws, per) == cols // nd)
    select[...] = hit.astype(F32).astype(BF16)

    across.wait_recv()
    for d in z_near:
        hand(0, partner, d, p_sems)

    row_id = lax.broadcasted_iota(jnp.int32, (LANES, LANES), 0)
    col_id = lax.broadcasted_iota(jnp.int32, (LANES, LANES), 1)
    eye = (row_id == col_id).astype(F32)
    left_half = lax.broadcasted_iota(jnp.int32, (1, LANES), 1) < R

    pltpu.make_async_copy(rs_buf, rs_buf, rs_sems[1]).wait()
    mine = part[f]
    for r in range(rs_buf.shape[0]):
        mine = mine + rs_buf[r]
    chunks[f] = mine

    zero = jnp.zeros_like(mine)
    wide = jnp.concatenate([jnp.where(side == 0, mine, zero), jnp.where(side == 0, zero, mine)], axis=0)
    gram = exact(mine, wide, NT)
    for t in range(ntb):
        gram_part[t] = gram[rows * t:rows * (t + 1)]

    for r in by_distance(range(1, ntb), f_far):
        to = lax.rem(block + r, ntb)
        send(gram_part.at[to], ga_buf.at[r - 1], ga_sems, {"fsdp": side * ntb + to})

    await_blocks(len(z_near), q_sems[1])
    await_blocks(len(z_near), p_sems[1])
    pltpu.make_async_copy(ga_buf, ga_buf, ga_sems[1]).wait()
    gsum = gram_part[block]
    for r in range(ntb - 1):
        gsum = gsum + ga_buf[r]
    gb_own[0] = gsum
    twin = send(gb_own.at[0], gs_buf, gs_sems, sibling)
    for d in far:
        send(chunks.at[f], chunks.at[f], far_sems, {"fsdp": place_of(col, d)})
    for d in near:
        for c in (other, col):
            send(chunks.at[f], chunks.at[f], ag_sems, {"fsdp": place_of(c, d)})
    send(chunks.at[f], chunks.at[f], ag_sems, pair_f)
    twin.wait_recv()
    gsum = gsum + gs_buf[...]
    gb_own[1] = gsum
    for r in d_steps:
        send(gb_own.at[1], gb_buf.at[r - 1], gb_sems, over_d(r))
    onward(x, q2_sems)
    onward(partner, p2_sems)
    far_chunks = chunks.at[pl.ds(0, len(far))]
    if far:
        pltpu.make_async_copy(far_chunks, far_chunks, far_sems[1]).wait()
    for d in far:
        held = chunks.at[place_of(col, d)]
        send(held, held, hand_sems, pair_f)

    pltpu.make_async_copy(gb_buf, gb_buf, gb_sems[1]).wait()
    for r in range(nch - 1):
        gsum = gsum + gb_buf[r]
    place = f
    gfull[place] = gsum

    for r in f_steps:
        send(gfull.at[place], gfull.at[place], gc_sems, over_f(r))


    near_chunks = chunks.at[pl.ds(0, 1 + 2 * len(near))]
    pltpu.make_async_copy(near_chunks, near_chunks, ag_sems[1]).wait()
    if far:
        pltpu.make_async_copy(far_chunks, far_chunks, hand_sems[1]).wait()
    u_high, u_low = halves(jnp.concatenate([chunks[t] for t in range(ntb)], axis=1))
    v_high, v_low = halves(jnp.concatenate([chunks[ntb + t] for t in range(ntb)], axis=1))
    v_both = jnp.concatenate([v_high, v_low], axis=0)
    load_ids.wait()
    ids = ids_ref[...]
    none = jnp.zeros_like(u_high)
    pair = EX // 2
    for p in range(pair):
        marks = [jnp.broadcast_to(ids == e, u_high.shape) for e in (p, p + pair)]
        masked_high = jnp.concatenate([jnp.where(m, u_high, none) for m in marks], axis=0)
        masked_low = jnp.concatenate([jnp.where(m, u_low, none) for m in marks], axis=0)
        top = bf_dot(v_both, masked_high, NT)
        stage[pl.ds(R * p, R), :] = top[:R] + top[R:] + bf_dot(v_high, masked_low, NT)

    await_blocks(len(z_rest), q2_sems[1])
    await_blocks(len(z_rest), p2_sems[1])
    twin_q = send(qall.at[core], qall.at[core], sib_sems, sibling)
    all_grams = gfull.at[pl.ds(0, nf - 1)]
    pltpu.make_async_copy(all_grams, all_grams, gc_sems[1]).wait()
    inv = inverse_pair(jnp.concatenate([gfull[t] for t in range(nf)], axis=0), eye, left_half, 1.0 / tokens_all)
    corner = jnp.where(jnp.logical_and(row_id < R, col_id < R), inv, 0.0)
    twice = corner + pltpu.roll(pltpu.roll(corner, R, 0), R, 1)
    right = three(stage[...], twice)
    right = jnp.concatenate([right[R * p:R * (p + 1)] for p in range(pair)], axis=1)
    both = three(inv[R:], jnp.concatenate([right, right], axis=0))
    for p in range(pair):
        stage[pl.ds(R * p, R), :] = both[:, LANES * p:LANES * (p + 1)]
    for i in range(R // 2):
        a = stage[pl.ds(2 * i, pair, stride=R), :]
        b = stage[pl.ds(2 * i + 1, pair, stride=R), :]
        low = jnp.where(left_half, a, pltpu.roll(b, R, 1))
        high = jnp.where(left_half, pltpu.roll(a, R, 1), b)
        big, small = halves(jnp.concatenate([low, high], axis=0))
        top, left = (2 * i * R) // half * 2 * EX, (2 * i * R) % half
        flat[pl.ds(top, EX), pl.ds(left, LANES)] = big
        flat[pl.ds(top + EX, EX), pl.ds(left, LANES)] = small

    twin_q.wait_recv()
    raw = bf_dot(flat[...], qall[...].reshape(nd * 2 * per, half), NT)
    first = raw[:EX] + raw[EX:2 * EX]
    second = raw[2 * EX:3 * EX] + raw[3 * EX:]
    column = lax.broadcasted_iota(jnp.int32, first.shape, 1)
    sums = jnp.where(lax.rem(column // per, 2) == 0, first, second)
    big = sums.astype(BF16)
    rest = sums - big.astype(F32)
    mid = rest.astype(BF16)
    tail = (rest - mid.astype(F32)).astype(BF16)
    picked = bf_dot(jnp.concatenate([big, mid, tail], axis=0), select[...])
    picked = (picked[:EX] + picked[EX:2 * EX] + picked[2 * EX:]) * (1.0 / (R * R))
    for i in range(per):
        out_ref[:, i, :] = picked[:, nd * i:nd * (i + 1)]

    across.wait_send()
    twin.wait_send()
    twin_q.wait_send()
    for buf, pair_sems in (
        (rs_buf, rs_sems), (near_chunks, ag_sems), (ga_buf, ga_sems), (gb_buf, gb_sems), (all_grams, gc_sems),
    ):
        pltpu.make_async_copy(buf, buf, pair_sems[0]).wait()
    if far:
        pltpu.make_async_copy(cross, cross, cross_sems[0]).wait()
        pltpu.make_async_copy(far_chunks, far_chunks, far_sems[0]).wait()
        pltpu.make_async_copy(far_chunks, far_chunks, hand_sems[0]).wait()
    for count, pair_sems in ((z_near, q_sems), (z_near, p_sems), (z_rest, q2_sems), (z_rest, p2_sems)):
        await_blocks(len(count), pair_sems[0])


def on_device(
    nf, nd, attn_out, key_cotangent, key_weight, proj_in, proj_out, query_sketches, block_owner, example_ids
):
    tokens = attn_out.shape[0]
    per = query_sketches.shape[1]
    half = query_sketches.shape[2] // 2
    ntb = nf // 2
    rows = R // ntb
    far = len(split_ring(ntb)[1])
    hbm = pl.BlockSpec(memory_space=pl.ANY)
    vmem = pl.BlockSpec(memory_space=pltpu.VMEM)
    scores = pl.pallas_call(
        functools.partial(kernel, nf, nd, nd * tokens),
        out_shape=jax.ShapeDtypeStruct((EX, per, nd), F32),
        in_specs=[hbm] * 8,
        out_specs=vmem,
        scratch_shapes=[
            pltpu.VMEM(attn_out.shape, BF16),
            pltpu.VMEM(key_cotangent.shape, BF16),
            pltpu.VMEM(key_weight.shape, BF16),
            pltpu.VMEM(proj_in.shape, BF16),
            pltpu.VMEM(proj_out.shape, BF16),
            pltpu.VMEM(query_sketches.shape, BF16),
            pltpu.VMEM((1, nd), jnp.int32),
            pltpu.VMEM(example_ids.shape, jnp.int32),
            pltpu.VMEM((nf, R, LANES), F32),
            pltpu.VMEM((max(1, far), R, LANES), F32),
            pltpu.VMEM((max(1, far), R, LANES), F32),
            pltpu.VMEM((nf - 1 - far, R, LANES), F32),
            pltpu.VMEM((nf, R, LANES), F32),
            pltpu.VMEM((ntb, rows, LANES), F32),
            pltpu.VMEM((ntb - 1, rows, LANES), F32),
            pltpu.VMEM((rows, LANES), F32),
            pltpu.VMEM((2, rows, LANES), F32),
            pltpu.VMEM((nd // 2 - 1, rows, LANES), F32),
            pltpu.VMEM((nf, rows, LANES), F32),
            pltpu.VMEM((2, nd // 4, 2, 2 * per, half), BF16),
            pltpu.VMEM((nd * 2 * per, per * nd), BF16),
            pltpu.VMEM((4 * EX, half), BF16),
            pltpu.VMEM((EX // 2 * R, LANES), F32),
            pltpu.SemaphoreType.DMA((8,)),
            pltpu.SemaphoreType.REGULAR,
        ] + [pltpu.SemaphoreType.DMA] * 30,
        compiler_params=pltpu.CompilerParams(
            collective_id=0, has_side_effects=True, vmem_limit_bytes=62 * 1024 * 1024
        ),
        name="influence",
    )(
        attn_out, key_cotangent, key_weight, proj_in, proj_out, query_sketches,
        block_owner.reshape(1, nd), example_ids,
    )
    return scores.transpose(0, 2, 1)


def solution(mesh):
    return jax.shard_map(
        functools.partial(on_device, mesh.shape["fsdp"], mesh.shape["dp"]),
        mesh=mesh,
        in_specs=(
            P("dp", "fsdp"),
            P("dp", None),
            P("fsdp", None),
            P(None, "fsdp"),
            P(None, "fsdp"),
            P("dp", "fsdp", None),
            P(),
            P("dp", None),
        ),
        out_specs=P("dp", None, "fsdp"),
        check_vma=False,
    )
```

```python
import functools
import jax
import jax.numpy as jnp
from jax import lax
from jax.experimental import pallas as pl
from jax.experimental.pallas import tpu as pltpu
from jax.sharding import PartitionSpec as P

EX = 16
R = 64
LANES = 128
MESH = pl.DeviceIdType.MESH
NT = (((1,), (1,)), ((), ()))
F32 = jnp.float32
BF16 = jnp.bfloat16


def exact(a, b, dims=(((1,), (0,)), ((), ()))):
    return lax.dot_general(a, b, dims, precision=lax.Precision.HIGHEST, preferred_element_type=F32)


def bf_dot(a, b, dims=(((1,), (0,)), ((), ()))):
    return lax.dot_general(a, b, dims, preferred_element_type=F32)


def halves(x):
    high = x.astype(BF16)
    return high, (x - high.astype(F32)).astype(BF16)


def three(a, b):
    a_high, a_low = halves(a)
    b_high, b_low = halves(b)
    return bf_dot(jnp.concatenate([a_high, a_low, a_high], axis=1), jnp.concatenate([b_high, b_high, b_low], axis=0))


def split_ring(n):
    near = [d for d in (n - 2, 2, n - 1, 1) if 0 < d < n]
    near = sorted(set(near), key=near.index)
    return near, [d for d in (n // 2, n // 2 - 1, n // 2 + 1) if 0 < d < n and d not in near]


def inverse_pair(gram, eye, left_half, scale):
    diag = jnp.sum(gram * eye, axis=0, keepdims=True) * scale
    tr_in = jnp.sum(jnp.where(left_half, diag, 0.0), axis=1, keepdims=True)
    tr_out = jnp.sum(jnp.where(left_half, 0.0, diag), axis=1, keepdims=True)
    bound = jnp.where(left_half, tr_in, tr_out) * (1.0 + 0.1 / R)
    low = (0.1 / R) / (1.0 + 0.1 / R)
    mat = gram * (scale / bound) + low * eye
    start = 2.0 / (1.0 + low)
    rho = (1.0 - low) / (1.0 + low)
    gain = 2.0 / (2.0 - rho * rho)
    rho = rho * rho / (2.0 - rho * rho)
    prod = start * mat
    turn = 2.0 * eye - prod
    inv = (gain * start) * turn
    prod = gain * three(prod, turn)
    while rho > 0.05:
        gain = 2.0 / (2.0 - rho * rho)
        rho = rho * rho / (2.0 - rho * rho)
        turn = 2.0 * eye - prod
        both = three(jnp.concatenate([prod, inv], axis=0), turn) * gain
        prod, inv = both[:LANES], both[LANES:]
    for _ in range(2):
        inv = inv + three(inv, eye - exact(mat, inv))
    return inv / bound


def by_distance(steps, far):
    return sorted(steps, key=lambda r: -far(r))


def kernel(
    nf, nd, tokens_all,
    attn_hbm, cot_hbm, kw_hbm, pin_hbm, pout_hbm, query_hbm, owner_hbm, ids_hbm,
    out_ref,
    attn, cot, kw, pin_ref, pout_ref, query_ref, owner_ref, ids_ref, part, cross, joint, rs_buf, chunks, gram_part, ga_buf, gs_buf, gb_own, gb_buf, gfull, qall, select, flat, stage,
    load_sem, relay, *sems,
):
    (
        rs_sems, cross_sems, ag_sems, far_sems, hand_sems, ga_sems, gs_sems, gb_sems, gc_sems,
        x_sems, q_sems, p_sems, q2_sems, p2_sems, sib_sems,
    ) = zip(sems[::2], sems[1::2])
    f = lax.axis_index("fsdp")
    j = lax.axis_index("dp")
    ntb = nf // 2
    nch = nd // 2
    rows = R // ntb
    core, chip = lax.rem(j, 2), j // 2
    side, block = f // ntb, lax.rem(f, ntb)
    half = query_ref.shape[2] // 2
    per = query_ref.shape[1]

    load_attn = pltpu.make_async_copy(attn_hbm, attn, load_sem.at[0])
    load_pin = pltpu.make_async_copy(pin_hbm, pin_ref, load_sem.at[1])
    load_kw = pltpu.make_async_copy(kw_hbm, kw, load_sem.at[2])
    load_pout = pltpu.make_async_copy(pout_hbm, pout_ref, load_sem.at[3])
    load_cot = pltpu.make_async_copy(cot_hbm, cot, load_sem.at[4])
    load_query = pltpu.make_async_copy(query_hbm, query_ref, load_sem.at[5])
    load_owner = pltpu.make_async_copy(owner_hbm, owner_ref, load_sem.at[6])
    load_ids = pltpu.make_async_copy(ids_hbm, ids_ref, load_sem.at[7])
    for load in (load_attn, load_pin, load_kw, load_pout, load_cot, load_query, load_owner, load_ids):
        load.start()

    ny, nz = nf // 2, nd // 4
    f_far = lambda r: min(r % ny, ny - r % ny) + (r >= ny)
    z_far = lambda r: min(r % nz, nz - r % nz) + 2 * (r >= nz)
    f_steps = by_distance(range(1, nf), f_far)
    d_steps = by_distance(range(1, nch), z_far)
    sibling = {"dp": j + 1 - 2 * core}
    over_f = lambda r: {"fsdp": lax.rem(f + r, nf)}
    over_d = lambda r: {"dp": lax.rem(j + 2 * r, nd)}

    col, y = f // ny, lax.rem(f, ny)
    place_of = lambda c, d: c * ny + lax.rem(y + d, ny)
    near, far = split_ring(ny)
    other = 1 - col
    pair_f = {"fsdp": place_of(other, 0)}
    z, x = lax.rem(chip, nz), chip // nz
    partner = 1 - x
    z_near, z_rest = split_ring(nz)
    over_z = lambda d: {"dp": (x * nz + lax.rem(z + d, nz)) * 2 + core}
    pair_d = {"dp": lax.rem(j + nch, nd)}
    greeted = [pair_f, pair_d, sibling] + [over_z(d) for d in z_near]
    greeted += [{"fsdp": place_of(c, d)} for d in near for c in (other, col)]
    barrier = pltpu.get_barrier_semaphore()
    for peer in reversed(greeted):
        pl.semaphore_signal(barrier, inc=1, device_id=peer, device_id_type=MESH)

    def send(src, dst, sems, peer):
        copy = pltpu.make_async_remote_copy(
            src_ref=src, dst_ref=dst, send_sem=sems[0], recv_sem=sems[1], device_id=peer, device_id_type=MESH
        )
        copy.start()
        return copy

    load_attn.wait()
    load_pin.wait()
    u_part = bf_dot(pin_ref[...], attn[...], NT)
    for t in range(ntb):
        part[t] = u_part[:, LANES * t:LANES * (t + 1)]

    load_kw.wait()
    load_pout.wait()
    w_part = bf_dot(pout_ref[...], kw[...])
    w_two = jnp.concatenate(halves(w_part), axis=0)
    load_cot.wait()
    v_two = bf_dot(w_two, cot[...], NT)
    v_part = v_two[:R] + v_two[R:]
    for t in range(ntb):
        part[ntb + t] = v_part[:, LANES * t:LANES * (t + 1)]
    pl.semaphore_wait(barrier, len(greeted))
    relays = [2, ny - 2] if far else []
    for d in relays:
        pl.semaphore_signal(relay, inc=1, device_id={"fsdp": place_of(col, d)}, device_id_type=MESH)

    for k, d in enumerate(far):
        send(part.at[place_of(other, d)], cross.at[k], cross_sems, pair_f)
    for k, d in enumerate(near):
        for i, c in enumerate((other, col)):
            to = place_of(c, d)
            send(part.at[to], rs_buf.at[1 + 2 * k + i], rs_sems, {"fsdp": to})
    send(part.at[place_of(other, 0)], rs_buf.at[0], rs_sems, pair_f)

    load_query.wait()
    own_q = query_ref[0]
    qall[core, z, x] = jnp.concatenate([own_q[:, :half], own_q[:, half:]], axis=0)
    across = send(qall.at[core, z, x], qall.at[core, z, x], x_sems, pair_d)

    def hand(origin, c, d, pair_sems):
        block = qall.at[core, lax.rem(z + origin, nz), c]
        send(block, block, pair_sems, over_z(d))

    def await_blocks(count, sem):
        if count:
            some = qall.at[0, pl.ds(0, count), 0]
            pltpu.make_async_copy(some, some, sem).wait()

    def onward(c, rest_sems):
        if z_rest:
            hand(nz - 2, c, 2, rest_sems)
            hand(nz - 2, c, 1, rest_sems)
            hand(2, c, nz - 1, rest_sems)

    for d in z_near:
        hand(0, x, d, q_sems)

    if far:
        pl.semaphore_wait(relay, len(relays))
        pltpu.make_async_copy(cross, cross, cross_sems[1]).wait()
    for k, d in enumerate(far):
        to = place_of(col, d)
        joint[k] = part[to] + cross[k]
        send(joint.at[k], rs_buf.at[1 + 2 * len(near) + k], rs_sems, {"fsdp": to})

    load_owner.wait()
    owner = jnp.concatenate([owner_ref[...]] * per, axis=1)
    cols = lax.broadcasted_iota(jnp.int32, select.shape, 1)
    rws = lax.broadcasted_iota(jnp.int32, select.shape, 0)
    block_of = rws // (2 * per)
    holder = (lax.rem(block_of, 2) * nz + lax.rem(block_of // 2, nz)) * 2 + block_of // nch
    hit = jnp.logical_and(holder == owner, lax.rem(rws, per) == cols // nd)
    select[...] = hit.astype(F32).astype(BF16)

    across.wait_recv()
    for d in z_near:
        hand(0, partner, d, p_sems)

    row_id = lax.broadcasted_iota(jnp.int32, (LANES, LANES), 0)
    col_id = lax.broadcasted_iota(jnp.int32, (LANES, LANES), 1)
    eye = (row_id == col_id).astype(F32)
    left_half = lax.broadcasted_iota(jnp.int32, (1, LANES), 1) < R

    pltpu.make_async_copy(rs_buf, rs_buf, rs_sems[1]).wait()
    mine = part[f]
    for r in range(rs_buf.shape[0]):
        mine = mine + rs_buf[r]
    chunks[f] = mine

    zero = jnp.zeros_like(mine)
    wide = jnp.concatenate([jnp.where(side == 0, mine, zero), jnp.where(side == 0, zero, mine)], axis=0)
    gram = exact(mine, wide, NT)
    for t in range(ntb):
        gram_part[t] = gram[rows * t:rows * (t + 1)]

    for r in by_distance(range(1, ntb), f_far):
        to = lax.rem(block + r, ntb)
        send(gram_part.at[to], ga_buf.at[r - 1], ga_sems, {"fsdp": side * ntb + to})

    await_blocks(len(z_near), q_sems[1])
    await_blocks(len(z_near), p_sems[1])
    pltpu.make_async_copy(ga_buf, ga_buf, ga_sems[1]).wait()
    gsum = gram_part[block]
    for r in range(ntb - 1):
        gsum = gsum + ga_buf[r]
    gb_own[0] = gsum
    twin = send(gb_own.at[0], gs_buf, gs_sems, sibling)
    for d in far:
        send(chunks.at[f], chunks.at[f], far_sems, {"fsdp": place_of(col, d)})
    twin.wait_recv()
    gsum = gsum + gs_buf[...]
    gb_own[1] = gsum
    for r in d_steps:
        send(gb_own.at[1], gb_buf.at[r - 1], gb_sems, over_d(r))
    for d in near:
        for c in (other, col):
            send(chunks.at[f], chunks.at[f], ag_sems, {"fsdp": place_of(c, d)})
    send(chunks.at[f], chunks.at[f], ag_sems, pair_f)
    onward(x, q2_sems)
    onward(partner, p2_sems)
    far_chunks = chunks.at[pl.ds(0, len(far))]
    if far:
        pltpu.make_async_copy(far_chunks, far_chunks, far_sems[1]).wait()
    for d in far:
        held = chunks.at[place_of(col, d)]
        send(held, held, hand_sems, pair_f)

    pltpu.make_async_copy(gb_buf, gb_buf, gb_sems[1]).wait()
    for r in range(nch - 1):
        gsum = gsum + gb_buf[r]
    place = f
    gfull[place] = gsum

    for r in f_steps:
        send(gfull.at[place], gfull.at[place], gc_sems, over_f(r))


    near_chunks = chunks.at[pl.ds(0, 1 + 2 * len(near))]
    pltpu.make_async_copy(near_chunks, near_chunks, ag_sems[1]).wait()
    if far:
        pltpu.make_async_copy(far_chunks, far_chunks, hand_sems[1]).wait()
    u_high, u_low = halves(jnp.concatenate([chunks[t] for t in range(ntb)], axis=1))
    v_high, v_low = halves(jnp.concatenate([chunks[ntb + t] for t in range(ntb)], axis=1))
    v_both = jnp.concatenate([v_high, v_low], axis=0)
    load_ids.wait()
    ids = ids_ref[...]
    none = jnp.zeros_like(u_high)
    pair = EX // 2
    for p in range(pair):
        marks = [jnp.broadcast_to(ids == e, u_high.shape) for e in (p, p + pair)]
        masked_high = jnp.concatenate([jnp.where(m, u_high, none) for m in marks], axis=0)
        masked_low = jnp.concatenate([jnp.where(m, u_low, none) for m in marks], axis=0)
        top = bf_dot(v_both, masked_high, NT)
        stage[pl.ds(R * p, R), :] = top[:R] + top[R:] + bf_dot(v_high, masked_low, NT)

    await_blocks(len(z_rest), q2_sems[1])
    await_blocks(len(z_rest), p2_sems[1])
    twin_q = send(qall.at[core], qall.at[core], sib_sems, sibling)
    all_grams = gfull.at[pl.ds(0, nf - 1)]
    pltpu.make_async_copy(all_grams, all_grams, gc_sems[1]).wait()
    inv = inverse_pair(jnp.concatenate([gfull[t] for t in range(nf)], axis=0), eye, left_half, 1.0 / tokens_all)
    corner = jnp.where(jnp.logical_and(row_id < R, col_id < R), inv, 0.0)
    twice = corner + pltpu.roll(pltpu.roll(corner, R, 0), R, 1)
    right = three(stage[...], twice)
    right = jnp.concatenate([right[R * p:R * (p + 1)] for p in range(pair)], axis=1)
    both = three(inv[R:], jnp.concatenate([right, right], axis=0))
    for p in range(pair):
        stage[pl.ds(R * p, R), :] = both[:, LANES * p:LANES * (p + 1)]
    for i in range(R // 2):
        a = stage[pl.ds(2 * i, pair, stride=R), :]
        b = stage[pl.ds(2 * i + 1, pair, stride=R), :]
        low = jnp.where(left_half, a, pltpu.roll(b, R, 1))
        high = jnp.where(left_half, pltpu.roll(a, R, 1), b)
        big, small = halves(jnp.concatenate([low, high], axis=0))
        top, left = (2 * i * R) // half * 2 * EX, (2 * i * R) % half
        flat[pl.ds(top, EX), pl.ds(left, LANES)] = big
        flat[pl.ds(top + EX, EX), pl.ds(left, LANES)] = small

    twin_q.wait_recv()
    raw = bf_dot(flat[...], qall[...].reshape(nd * 2 * per, half), NT)
    first = raw[:EX] + raw[EX:2 * EX]
    second = raw[2 * EX:3 * EX] + raw[3 * EX:]
    column = lax.broadcasted_iota(jnp.int32, first.shape, 1)
    sums = jnp.where(lax.rem(column // per, 2) == 0, first, second)
    big = sums.astype(BF16)
    rest = sums - big.astype(F32)
    mid = rest.astype(BF16)
    tail = (rest - mid.astype(F32)).astype(BF16)
    picked = bf_dot(jnp.concatenate([big, mid, tail], axis=0), select[...])
    picked = (picked[:EX] + picked[EX:2 * EX] + picked[2 * EX:]) * (1.0 / (R * R))
    for i in range(per):
        out_ref[:, i, :] = picked[:, nd * i:nd * (i + 1)]

    across.wait_send()
    twin.wait_send()
    twin_q.wait_send()
    for buf, pair_sems in (
        (rs_buf, rs_sems), (near_chunks, ag_sems), (ga_buf, ga_sems), (gb_buf, gb_sems), (all_grams, gc_sems),
    ):
        pltpu.make_async_copy(buf, buf, pair_sems[0]).wait()
    if far:
        pltpu.make_async_copy(cross, cross, cross_sems[0]).wait()
        pltpu.make_async_copy(far_chunks, far_chunks, far_sems[0]).wait()
        pltpu.make_async_copy(far_chunks, far_chunks, hand_sems[0]).wait()
    for count, pair_sems in ((z_near, q_sems), (z_near, p_sems), (z_rest, q2_sems), (z_rest, p2_sems)):
        await_blocks(len(count), pair_sems[0])


def on_device(
    nf, nd, attn_out, key_cotangent, key_weight, proj_in, proj_out, query_sketches, block_owner, example_ids
):
    tokens = attn_out.shape[0]
    per = query_sketches.shape[1]
    half = query_sketches.shape[2] // 2
    ntb = nf // 2
    rows = R // ntb
    far = len(split_ring(ntb)[1])
    hbm = pl.BlockSpec(memory_space=pl.ANY)
    vmem = pl.BlockSpec(memory_space=pltpu.VMEM)
    scores = pl.pallas_call(
        functools.partial(kernel, nf, nd, nd * tokens),
        out_shape=jax.ShapeDtypeStruct((EX, per, nd), F32),
        in_specs=[hbm] * 8,
        out_specs=vmem,
        scratch_shapes=[
            pltpu.VMEM(attn_out.shape, BF16),
            pltpu.VMEM(key_cotangent.shape, BF16),
            pltpu.VMEM(key_weight.shape, BF16),
            pltpu.VMEM(proj_in.shape, BF16),
            pltpu.VMEM(proj_out.shape, BF16),
            pltpu.VMEM(query_sketches.shape, BF16),
            pltpu.VMEM((1, nd), jnp.int32),
            pltpu.VMEM(example_ids.shape, jnp.int32),
            pltpu.VMEM((nf, R, LANES), F32),
            pltpu.VMEM((max(1, far), R, LANES), F32),
            pltpu.VMEM((max(1, far), R, LANES), F32),
            pltpu.VMEM((nf - 1 - far, R, LANES), F32),
            pltpu.VMEM((nf, R, LANES), F32),
            pltpu.VMEM((ntb, rows, LANES), F32),
            pltpu.VMEM((ntb - 1, rows, LANES), F32),
            pltpu.VMEM((rows, LANES), F32),
            pltpu.VMEM((2, rows, LANES), F32),
            pltpu.VMEM((nd // 2 - 1, rows, LANES), F32),
            pltpu.VMEM((nf, rows, LANES), F32),
            pltpu.VMEM((2, nd // 4, 2, 2 * per, half), BF16),
            pltpu.VMEM((nd * 2 * per, per * nd), BF16),
            pltpu.VMEM((4 * EX, half), BF16),
            pltpu.VMEM((EX // 2 * R, LANES), F32),
            pltpu.SemaphoreType.DMA((8,)),
            pltpu.SemaphoreType.REGULAR,
        ] + [pltpu.SemaphoreType.DMA] * 30,
        compiler_params=pltpu.CompilerParams(
            collective_id=0, has_side_effects=True, vmem_limit_bytes=62 * 1024 * 1024
        ),
        name="influence",
    )(
        attn_out, key_cotangent, key_weight, proj_in, proj_out, query_sketches,
        block_owner.reshape(1, nd), example_ids,
    )
    return scores.transpose(0, 2, 1)


def solution(mesh):
    return jax.shard_map(
        functools.partial(on_device, mesh.shape["fsdp"], mesh.shape["dp"]),
        mesh=mesh,
        in_specs=(
            P("dp", "fsdp"),
            P("dp", None),
            P("fsdp", None),
            P(None, "fsdp"),
            P(None, "fsdp"),
            P("dp", "fsdp", None),
            P(),
            P("dp", None),
        ),
        out_specs=P("dp", None, "fsdp"),
        check_vma=False,
    )
```

```python
import functools
import jax
import jax.numpy as jnp
from jax import lax
from jax.experimental import pallas as pl
from jax.experimental.pallas import tpu as pltpu
from jax.sharding import PartitionSpec as P

EX = 16
R = 64
LANES = 128
MESH = pl.DeviceIdType.MESH
NT = (((1,), (1,)), ((), ()))
F32 = jnp.float32
BF16 = jnp.bfloat16


def exact(a, b, dims=(((1,), (0,)), ((), ()))):
    return lax.dot_general(a, b, dims, precision=lax.Precision.HIGHEST, preferred_element_type=F32)


def bf_dot(a, b, dims=(((1,), (0,)), ((), ()))):
    return lax.dot_general(a, b, dims, preferred_element_type=F32)


def halves(x):
    high = x.astype(BF16)
    return high, (x - high.astype(F32)).astype(BF16)


def three(a, b):
    a_high, a_low = halves(a)
    b_high, b_low = halves(b)
    return bf_dot(jnp.concatenate([a_high, a_low, a_high], axis=1), jnp.concatenate([b_high, b_high, b_low], axis=0))


def split_ring(n):
    near = [d for d in (n - 2, 2, n - 1, 1) if 0 < d < n]
    near = sorted(set(near), key=near.index)
    return near, [d for d in (n // 2, n // 2 - 1, n // 2 + 1) if 0 < d < n and d not in near]


def inverse_pair(gram, eye, left_half, scale):
    diag = jnp.sum(gram * eye, axis=0, keepdims=True) * scale
    tr_in = jnp.sum(jnp.where(left_half, diag, 0.0), axis=1, keepdims=True)
    tr_out = jnp.sum(jnp.where(left_half, 0.0, diag), axis=1, keepdims=True)
    bound = jnp.where(left_half, tr_in, tr_out) * (1.0 + 0.1 / R)
    low = (0.1 / R) / (1.0 + 0.1 / R)
    mat = gram * (scale / bound) + low * eye
    start = 2.0 / (1.0 + low)
    rho = (1.0 - low) / (1.0 + low)
    gain = 2.0 / (2.0 - rho * rho)
    rho = rho * rho / (2.0 - rho * rho)
    prod = start * mat
    turn = 2.0 * eye - prod
    inv = (gain * start) * turn
    prod = gain * three(prod, turn)
    while rho > 0.05:
        gain = 2.0 / (2.0 - rho * rho)
        rho = rho * rho / (2.0 - rho * rho)
        turn = 2.0 * eye - prod
        both = three(jnp.concatenate([prod, inv], axis=0), turn) * gain
        prod, inv = both[:LANES], both[LANES:]
    for _ in range(2):
        inv = inv + three(inv, eye - exact(mat, inv))
    return inv / bound


def by_distance(steps, far):
    return sorted(steps, key=lambda r: -far(r))


def kernel(
    nf, nd, tokens_all,
    attn_hbm, cot_hbm, kw_hbm, pin_hbm, pout_hbm, query_hbm, owner_hbm, ids_hbm,
    out_ref,
    attn, cot, kw, pin_ref, pout_ref, query_ref, owner_ref, ids_ref, part, cross, joint, rs_buf, chunks, gram_part, ga_buf, gs_buf, gb_own, gb_buf, gfull, qall, select, flat, stage,
    load_sem, relay, *sems,
):
    (
        rs_sems, cross_sems, ag_sems, far_sems, hand_sems, ga_sems, gs_sems, gb_sems, gc_sems,
        x_sems, q_sems, p_sems, q2_sems, p2_sems, sib_sems,
    ) = zip(sems[::2], sems[1::2])
    f = lax.axis_index("fsdp")
    j = lax.axis_index("dp")
    ntb = nf // 2
    nch = nd // 2
    rows = R // ntb
    core, chip = lax.rem(j, 2), j // 2
    side, block = f // ntb, lax.rem(f, ntb)
    half = query_ref.shape[2] // 2
    per = query_ref.shape[1]

    load_attn = pltpu.make_async_copy(attn_hbm, attn, load_sem.at[0])
    load_pin = pltpu.make_async_copy(pin_hbm, pin_ref, load_sem.at[1])
    load_kw = pltpu.make_async_copy(kw_hbm, kw, load_sem.at[2])
    load_pout = pltpu.make_async_copy(pout_hbm, pout_ref, load_sem.at[3])
    load_cot = pltpu.make_async_copy(cot_hbm, cot, load_sem.at[4])
    load_query = pltpu.make_async_copy(query_hbm, query_ref, load_sem.at[5])
    load_owner = pltpu.make_async_copy(owner_hbm, owner_ref, load_sem.at[6])
    load_ids = pltpu.make_async_copy(ids_hbm, ids_ref, load_sem.at[7])
    for load in (load_attn, load_pin, load_kw, load_pout, load_cot, load_query, load_owner, load_ids):
        load.start()

    ny, nz = nf // 2, nd // 4
    f_far = lambda r: min(r % ny, ny - r % ny) + (r >= ny)
    z_far = lambda r: min(r % nz, nz - r % nz) + 2 * (r >= nz)
    f_steps = by_distance(range(1, nf), f_far)
    d_steps = by_distance(range(1, nch), z_far)
    sibling = {"dp": j + 1 - 2 * core}
    over_f = lambda r: {"fsdp": lax.rem(f + r, nf)}
    over_d = lambda r: {"dp": lax.rem(j + 2 * r, nd)}

    col, y = f // ny, lax.rem(f, ny)
    place_of = lambda c, d: c * ny + lax.rem(y + d, ny)
    near, far = split_ring(ny)
    other = 1 - col
    pair_f = {"fsdp": place_of(other, 0)}
    z, x = lax.rem(chip, nz), chip // nz
    partner = 1 - x
    z_near, z_rest = split_ring(nz)
    over_z = lambda d: {"dp": (x * nz + lax.rem(z + d, nz)) * 2 + core}
    pair_d = {"dp": lax.rem(j + nch, nd)}
    greeted = [pair_f, pair_d, sibling] + [over_z(d) for d in z_near]
    greeted += [{"fsdp": place_of(c, d)} for d in near for c in (other, col)]
    barrier = pltpu.get_barrier_semaphore()
    for peer in reversed(greeted):
        pl.semaphore_signal(barrier, inc=1, device_id=peer, device_id_type=MESH)

    def send(src, dst, sems, peer):
        copy = pltpu.make_async_remote_copy(
            src_ref=src, dst_ref=dst, send_sem=sems[0], recv_sem=sems[1], device_id=peer, device_id_type=MESH
        )
        copy.start()
        return copy

    load_attn.wait()
    load_pin.wait()
    u_part = bf_dot(pin_ref[...], attn[...], NT)
    for t in range(ntb):
        part[t] = u_part[:, LANES * t:LANES * (t + 1)]

    load_kw.wait()
    load_pout.wait()
    w_part = bf_dot(pout_ref[...], kw[...])
    w_two = jnp.concatenate(halves(w_part), axis=0)
    load_cot.wait()
    v_two = bf_dot(w_two, cot[...], NT)
    v_part = v_two[:R] + v_two[R:]
    for t in range(ntb):
        part[ntb + t] = v_part[:, LANES * t:LANES * (t + 1)]
    pl.semaphore_wait(barrier, len(greeted))
    relays = [2, ny - 2] if far else []
    for d in relays:
        pl.semaphore_signal(relay, inc=1, device_id={"fsdp": place_of(col, d)}, device_id_type=MESH)

    for k, d in enumerate(far):
        send(part.at[place_of(other, d)], cross.at[k], cross_sems, pair_f)
    for k, d in enumerate(near):
        for i, c in enumerate((other, col)):
            to = place_of(c, d)
            send(part.at[to], rs_buf.at[1 + 2 * k + i], rs_sems, {"fsdp": to})
    send(part.at[place_of(other, 0)], rs_buf.at[0], rs_sems, pair_f)

    load_query.wait()
    own_q = query_ref[0]
    qall[core, z, x] = jnp.concatenate([own_q[:, :half], own_q[:, half:]], axis=0)
    across = send(qall.at[core, z, x], qall.at[core, z, x], x_sems, pair_d)

    def hand(origin, c, d, pair_sems):
        block = qall.at[core, lax.rem(z + origin, nz), c]
        send(block, block, pair_sems, over_z(d))

    def await_blocks(count, sem):
        if count:
            some = qall.at[0, pl.ds(0, count), 0]
            pltpu.make_async_copy(some, some, sem).wait()

    def onward(c, rest_sems):
        if z_rest:
            hand(nz - 2, c, 2, rest_sems)
            hand(nz - 2, c, 1, rest_sems)
            hand(2, c, nz - 1, rest_sems)

    for d in z_near:
        hand(0, x, d, q_sems)

    if far:
        pl.semaphore_wait(relay, len(relays))
        pltpu.make_async_copy(cross, cross, cross_sems[1]).wait()
    for k, d in enumerate(far):
        to = place_of(col, d)
        joint[k] = part[to] + cross[k]
        send(joint.at[k], rs_buf.at[1 + 2 * len(near) + k], rs_sems, {"fsdp": to})

    load_owner.wait()
    owner = jnp.concatenate([owner_ref[...]] * per, axis=1)
    cols = lax.broadcasted_iota(jnp.int32, select.shape, 1)
    rws = lax.broadcasted_iota(jnp.int32, select.shape, 0)
    block_of = rws // (2 * per)
    holder = (lax.rem(block_of, 2) * nz + lax.rem(block_of // 2, nz)) * 2 + block_of // nch
    hit = jnp.logical_and(holder == owner, lax.rem(rws, per) == cols // nd)
    select[...] = hit.astype(F32).astype(BF16)

    across.wait_recv()
    for d in z_near:
        hand(0, partner, d, p_sems)

    row_id = lax.broadcasted_iota(jnp.int32, (LANES, LANES), 0)
    col_id = lax.broadcasted_iota(jnp.int32, (LANES, LANES), 1)
    eye = (row_id == col_id).astype(F32)
    left_half = lax.broadcasted_iota(jnp.int32, (1, LANES), 1) < R

    pltpu.make_async_copy(rs_buf, rs_buf, rs_sems[1]).wait()
    mine = part[f]
    for r in range(rs_buf.shape[0]):
        mine = mine + rs_buf[r]
    chunks[f] = mine

    zero = jnp.zeros_like(mine)
    wide = jnp.concatenate([jnp.where(side == 0, mine, zero), jnp.where(side == 0, zero, mine)], axis=0)
    gram = exact(mine, wide, NT)
    for t in range(ntb):
        gram_part[t] = gram[rows * t:rows * (t + 1)]

    for r in by_distance(range(1, ntb), f_far):
        to = lax.rem(block + r, ntb)
        send(gram_part.at[to], ga_buf.at[r - 1], ga_sems, {"fsdp": side * ntb + to})

    await_blocks(len(z_near), q_sems[1])
    await_blocks(len(z_near), p_sems[1])
    pltpu.make_async_copy(ga_buf, ga_buf, ga_sems[1]).wait()
    gsum = gram_part[block]
    for r in range(ntb - 1):
        gsum = gsum + ga_buf[r]
    gb_own[0] = gsum
    twin = send(gb_own.at[0], gs_buf, gs_sems, sibling)
    for d in far:
        send(chunks.at[f], chunks.at[f], far_sems, {"fsdp": place_of(col, d)})
    twin.wait_recv()
    gsum = gsum + gs_buf[...]
    gb_own[1] = gsum
    for r in d_steps:
        send(gb_own.at[1], gb_buf.at[r - 1], gb_sems, over_d(r))
    for d in near:
        for c in (other, col):
            send(chunks.at[f], chunks.at[f], ag_sems, {"fsdp": place_of(c, d)})
    send(chunks.at[f], chunks.at[f], ag_sems, pair_f)
    onward(x, q2_sems)
    onward(partner, p2_sems)
    far_chunks = chunks.at[pl.ds(0, len(far))]
    if far:
        pltpu.make_async_copy(far_chunks, far_chunks, far_sems[1]).wait()
    for d in far:
        held = chunks.at[place_of(col, d)]
        send(held, held, hand_sems, pair_f)

    pltpu.make_async_copy(gb_buf, gb_buf, gb_sems[1]).wait()
    for r in range(nch - 1):
        gsum = gsum + gb_buf[r]
    place = f
    gfull[place] = gsum

    for r in f_steps:
        send(gfull.at[place], gfull.at[place], gc_sems, over_f(r))


    near_chunks = chunks.at[pl.ds(0, 1 + 2 * len(near))]
    pltpu.make_async_copy(near_chunks, near_chunks, ag_sems[1]).wait()
    if far:
        pltpu.make_async_copy(far_chunks, far_chunks, hand_sems[1]).wait()
    u_high, u_low = halves(jnp.concatenate([chunks[t] for t in range(ntb)], axis=1))
    v_high, v_low = halves(jnp.concatenate([chunks[ntb + t] for t in range(ntb)], axis=1))
    v_both = jnp.concatenate([v_high, v_low], axis=0)
    load_ids.wait()
    ids = ids_ref[...]
    none = jnp.zeros_like(u_high)
    pair = EX // 2
    for p in range(pair):
        marks = [jnp.broadcast_to(ids == e, u_high.shape) for e in (p, p + pair)]
        masked_high = jnp.concatenate([jnp.where(m, u_high, none) for m in marks], axis=0)
        masked_low = jnp.concatenate([jnp.where(m, u_low, none) for m in marks], axis=0)
        top = bf_dot(v_both, masked_high, NT)
        stage[pl.ds(R * p, R), :] = top[:R] + top[R:] + bf_dot(v_high, masked_low, NT)

    await_blocks(len(z_rest), q2_sems[1])
    await_blocks(len(z_rest), p2_sems[1])
    twin_q = send(qall.at[core], qall.at[core], sib_sems, sibling)
    all_grams = gfull.at[pl.ds(0, nf - 1)]
    pltpu.make_async_copy(all_grams, all_grams, gc_sems[1]).wait()
    inv = inverse_pair(jnp.concatenate([gfull[t] for t in range(nf)], axis=0), eye, left_half, 1.0 / tokens_all)
    corner = jnp.where(jnp.logical_and(row_id < R, col_id < R), inv, 0.0)
    twice = corner + pltpu.roll(pltpu.roll(corner, R, 0), R, 1)
    right = three(stage[...], twice)
    right = jnp.concatenate([right[R * p:R * (p + 1)] for p in range(pair)], axis=1)
    both = three(inv[R:], jnp.concatenate([right, right], axis=0))
    for p in range(pair):
        stage[pl.ds(R * p, R), :] = both[:, LANES * p:LANES * (p + 1)]
    for i in range(R // 2):
        a = stage[pl.ds(2 * i, pair, stride=R), :]
        b = stage[pl.ds(2 * i + 1, pair, stride=R), :]
        low = jnp.where(left_half, a, pltpu.roll(b, R, 1))
        high = jnp.where(left_half, pltpu.roll(a, R, 1), b)
        big, small = halves(jnp.concatenate([low, high], axis=0))
        top, left = (2 * i * R) // half * 2 * EX, (2 * i * R) % half
        flat[pl.ds(top, EX), pl.ds(left, LANES)] = big
        flat[pl.ds(top + EX, EX), pl.ds(left, LANES)] = small

    twin_q.wait_recv()
    raw = bf_dot(flat[...], qall[...].reshape(nd * 2 * per, half), NT)
    first = raw[:EX] + raw[EX:2 * EX]
    second = raw[2 * EX:3 * EX] + raw[3 * EX:]
    column = lax.broadcasted_iota(jnp.int32, first.shape, 1)
    sums = jnp.where(lax.rem(column // per, 2) == 0, first, second)
    big = sums.astype(BF16)
    rest = sums - big.astype(F32)
    mid = rest.astype(BF16)
    tail = (rest - mid.astype(F32)).astype(BF16)
    picked = bf_dot(jnp.concatenate([big, mid, tail], axis=0), select[...])
    picked = (picked[:EX] + picked[EX:2 * EX] + picked[2 * EX:]) * (1.0 / (R * R))
    out_ref[...] = picked

    across.wait_send()
    twin.wait_send()
    twin_q.wait_send()
    for buf, pair_sems in (
        (rs_buf, rs_sems), (near_chunks, ag_sems), (ga_buf, ga_sems), (gb_buf, gb_sems), (all_grams, gc_sems),
    ):
        pltpu.make_async_copy(buf, buf, pair_sems[0]).wait()
    if far:
        pltpu.make_async_copy(cross, cross, cross_sems[0]).wait()
        pltpu.make_async_copy(far_chunks, far_chunks, far_sems[0]).wait()
        pltpu.make_async_copy(far_chunks, far_chunks, hand_sems[0]).wait()
    for count, pair_sems in ((z_near, q_sems), (z_near, p_sems), (z_rest, q2_sems), (z_rest, p2_sems)):
        await_blocks(len(count), pair_sems[0])


def on_device(
    nf, nd, attn_out, key_cotangent, key_weight, proj_in, proj_out, query_sketches, block_owner, example_ids
):
    tokens = attn_out.shape[0]
    per = query_sketches.shape[1]
    half = query_sketches.shape[2] // 2
    ntb = nf // 2
    rows = R // ntb
    far = len(split_ring(ntb)[1])
    hbm = pl.BlockSpec(memory_space=pl.ANY)
    vmem = pl.BlockSpec(memory_space=pltpu.VMEM)
    scores = pl.pallas_call(
        functools.partial(kernel, nf, nd, nd * tokens),
        out_shape=jax.ShapeDtypeStruct((EX, per * nd), F32),
        in_specs=[hbm] * 8,
        out_specs=vmem,
        scratch_shapes=[
            pltpu.VMEM(attn_out.shape, BF16),
            pltpu.VMEM(key_cotangent.shape, BF16),
            pltpu.VMEM(key_weight.shape, BF16),
            pltpu.VMEM(proj_in.shape, BF16),
            pltpu.VMEM(proj_out.shape, BF16),
            pltpu.VMEM(query_sketches.shape, BF16),
            pltpu.VMEM((1, nd), jnp.int32),
            pltpu.VMEM(example_ids.shape, jnp.int32),
            pltpu.VMEM((nf, R, LANES), F32),
            pltpu.VMEM((max(1, far), R, LANES), F32),
            pltpu.VMEM((max(1, far), R, LANES), F32),
            pltpu.VMEM((nf - 1 - far, R, LANES), F32),
            pltpu.VMEM((nf, R, LANES), F32),
            pltpu.VMEM((ntb, rows, LANES), F32),
            pltpu.VMEM((ntb - 1, rows, LANES), F32),
            pltpu.VMEM((rows, LANES), F32),
            pltpu.VMEM((2, rows, LANES), F32),
            pltpu.VMEM((nd // 2 - 1, rows, LANES), F32),
            pltpu.VMEM((nf, rows, LANES), F32),
            pltpu.VMEM((2, nd // 4, 2, 2 * per, half), BF16),
            pltpu.VMEM((nd * 2 * per, per * nd), BF16),
            pltpu.VMEM((4 * EX, half), BF16),
            pltpu.VMEM((EX // 2 * R, LANES), F32),
            pltpu.SemaphoreType.DMA((8,)),
            pltpu.SemaphoreType.REGULAR,
        ] + [pltpu.SemaphoreType.DMA] * 30,
        compiler_params=pltpu.CompilerParams(
            collective_id=0, has_side_effects=True, vmem_limit_bytes=62 * 1024 * 1024
        ),
        name="influence",
    )(
        attn_out, key_cotangent, key_weight, proj_in, proj_out, query_sketches,
        block_owner.reshape(1, nd), example_ids,
    )
    return scores.reshape(EX, per, nd).transpose(0, 2, 1)


def solution(mesh):
    return jax.shard_map(
        functools.partial(on_device, mesh.shape["fsdp"], mesh.shape["dp"]),
        mesh=mesh,
        in_specs=(
            P("dp", "fsdp"),
            P("dp", None),
            P("fsdp", None),
            P(None, "fsdp"),
            P(None, "fsdp"),
            P("dp", "fsdp", None),
            P(),
            P("dp", None),
        ),
        out_specs=P("dp", None, "fsdp"),
        check_vma=False,
    )
```
